32 devices in a mesh: dom: 8 (over z, x), sub: 4 (over y, core).
Axes of the slice: x: 2, y: 2, z: 4, core: 2. Of those that a mesh axis runs over, the one named last changes fastest.
Arguments:
- state: float32 [5, 64, 1024], P(None, None, ('dom', 'sub')), may hold values from -0.9 to 0.9
- adjoint_final: float32 [5, 64, 1024], P(None, None, ('dom', 'sub')), may hold values from -6 to 6
- send_slot: int32 [32, 192], P(('dom', 'sub')), may hold values from 0 to 192, as said below
- ext_index: int32 [6, 1024], P(None, ('dom', 'sub')), may hold values from 0 to 384, as said below
- ext_perm: int32 [6, 1024], P(None, ('dom', 'sub')), may hold values from 0 to 7
Outputs:
- state_end: float32 [5, 64, 1024], P(None, None, ('dom', 'sub'))
- adjoint_start: float32 [5, 64, 1024], P(None, None, ('dom', 'sub'))
The draws below stay inside these ranges and needn't reach their ends.
Inputs may be any that keep to these rules, and one draw needn't show every extreme that they name: `send_slot`: A value of 192 marks an empty slot, which carries zeros; the share of occupied slots differs from device to device, and device 0 fills all its slots. `ext_index`: values below 192 name a face of the same device, values from 192 to 383 a received slot, and 384 a wall.
All inputs are finite; a program needn't handle non-finite values.
Results may differ from the reference program's by a relative error of at most 0.0006.
Values may be sent and summed in bfloat16 or wider, within the bound.
A program may use at most 64 MiB of HBM per device.

```python
import jax
import jax.numpy as jnp
import numpy as np
from jax import lax

VARS = 5
NODES = 64
E_DEV = 32
SLOTS = 192
ELEMS = 1024
N_DOM = 8
N_SUB = 4
DEVICES = 32


def draw_send_slot(key, part):
    key = jax.random.fold_in(key, 11)
    first_key, second_key, third_key = jax.random.split(key, 3)
    fill_level = jax.random.randint(first_key, (DEVICES, 1), 30, 101)
    fill_level = jnp.where(jnp.arange(DEVICES)[:, None] == 0, 100, fill_level)
    occupied = jax.random.randint(second_key, (DEVICES, SLOTS), 0, 100) < fill_level
    faces = jax.random.randint(third_key, (DEVICES, SLOTS), 0, 6 * E_DEV)
    return jnp.where(occupied, faces, 6 * E_DEV).astype(jnp.int32)


def draw_ext_index(key, part):
    key = jax.random.fold_in(key, 23)
    first_key, second_key, third_key = jax.random.split(key, 3)
    selector = jax.random.randint(first_key, (6, ELEMS), 0, 100)
    local_face = jax.random.randint(second_key, (6, ELEMS), 0, 6 * E_DEV)
    remote_slot = 6 * E_DEV + jax.random.randint(third_key, (6, ELEMS), 0, SLOTS)
    wall_value = 6 * E_DEV + SLOTS
    chosen = jnp.where(selector < 10, wall_value, jnp.where(selector < 30, remote_slot, local_face))
    return chosen.astype(jnp.int32)


def set_ends(values, key, smallest, high):
    shape = values.shape
    place = [jax.random.randint(jax.random.fold_in(key, axis), (), 0, shape[axis]) for axis in range(len(shape))]
    values = values.at[tuple(place)].set(smallest)
    longest = shape.index(max(shape))
    place[longest] = (place[longest] + 1) % shape[longest]
    return values.at[tuple(place)].set(high)


def steps_of(key, extent, pieces, least, high):
    factor_of = 1.0
    for axis_at, shards_of in pieces:
        steps = jax.random.uniform(jax.random.fold_in(jax.random.fold_in(key, 6), axis_at), (shards_of,), jnp.float32, least / len(pieces), high / len(pieces))
        factor_of = factor_of * jnp.repeat(jnp.exp(steps), extent[axis_at] // shards_of).reshape((-1,) + (1,) * (len(extent) - 1 - axis_at))
    return factor_of


def bell_draw(rng, extent, scale, most, cuts=(), kind=jnp.bfloat16):
    drawn = scale * jax.random.normal(rng, extent, jnp.float32)
    if cuts:
        drawn = drawn * steps_of(rng, extent, cuts, -0.22, 0.18)
    return jnp.clip(drawn, -most, most).astype(kind)


def setup_inputs(seed: int = 0) -> dict:
    seeds = jax.random.split(jax.random.key(seed), 6)
    state = bell_draw(seeds[0], (VARS, NODES, ELEMS), 0.3, 0.9, ((2, 32),), jnp.float32)
    adjoint_final = bell_draw(seeds[1], (VARS, NODES, ELEMS), 1.0, 6.0, ((2, 32),), jnp.float32)
    send_slot = draw_send_slot(jax.random.fold_in(seeds[5], 71), 0)
    ext_index = draw_ext_index(jax.random.fold_in(seeds[5], 71), 0)
    ext_perm = set_ends(jax.random.randint(seeds[4], (6, ELEMS), 0, 8), jax.random.fold_in(seeds[4], 1), 0, 7).astype(jnp.int32)
    return dict(state=state, adjoint_final=adjoint_final, send_slot=send_slot, ext_index=ext_index, ext_perm=ext_perm)


step_size = 0.02
mean_flow = 0.3
penalty = 2.0
metric = 2.0
lift_factor = 12.0

def derivative_table():
    points = np.array([-1.0, -1.0 / np.sqrt(5.0), 1.0 / np.sqrt(5.0), 1.0])
    products = np.array([np.prod([points[target] - points[source] for source in range(4) if source != target]) for target in range(4)])
    result = np.zeros((4, 4))
    for target in range(4):
        for source in range(4):
            if target != source:
                result[target, source] = products[target] / (products[source] * (points[target] - points[source]))
        result[target, target] = -np.sum(result[target])
    return result.astype(np.float32)

def symmetry_table():
    result = np.zeros((8, 16), np.int32)
    for symmetry in range(8):
        layout = np.arange(16).reshape(4, 4)
        if symmetry & 4:
            layout = layout.T
        if symmetry & 1:
            layout = layout[::-1]
        if symmetry & 2:
            layout = layout[:, ::-1]
        result[symmetry] = layout.reshape(-1)
    return result

def normal_table():
    result = np.zeros((3, 6), np.float32)
    for facet in range(6):
        result[facet // 2, facet] = 2.0 * (facet % 2) - 1.0
    return result

def flux_along(fields, drift, normal_speed, pressure_weights):
    density = fields[0]
    pressure = fields[4]
    components = [drift * density + (1.0 + density) * normal_speed]
    for member in range(3):
        velocity = fields[1 + member]
        components.append(drift * velocity + velocity * normal_speed + pressure_weights[member] * pressure)
    components.append(drift * pressure + (1.0 + pressure) * normal_speed)
    return jnp.stack(components)

def volume_term(field):
    elements = field.shape[2]
    derivative = derivative_table()
    forms = ['ai,vijke->vajke', 'aj,vijke->viake', 'ak,vijke->vijae']
    total = jnp.zeros((5, 4, 4, 4, elements), jnp.float32)
    for direction in range(3):
        drift = mean_flow if direction == 0 else 0.0
        weights = [1.0 if member == direction else 0.0 for member in range(3)]
        flux = flux_along(field, drift, field[1 + direction], weights).reshape(5, 4, 4, 4, elements)
        total = total + jnp.einsum(forms[direction], jnp.asarray(derivative, jnp.float32), flux, precision=lax.Precision.HIGHEST)
    return -metric * total.reshape(5, 64, elements)

def normal_flux(trace):
    normals = normal_table()
    weights = [jnp.asarray(normals[member], jnp.float32)[:, None] for member in range(3)]
    normal_speed = weights[0] * trace[1] + weights[1] * trace[2] + weights[2] * trace[3]
    return flux_along(trace, mean_flow * weights[0], normal_speed, weights)

def face_traces(field):
    elements = field.shape[2]
    cube = field.reshape(5, 4, 4, 4, elements)
    surfaces = [cube[:, 0], cube[:, 3], cube[:, :, 0], cube[:, :, 3], cube[:, :, :, 0], cube[:, :, :, 3]]
    return jnp.stack([surface.reshape(5, 16, elements) for surface in surfaces], axis=2).reshape(5, 16, 6 * elements)

def pack_sends(field, slots, n_sub):
    traces = face_traces(field)
    padded = jnp.concatenate([traces, jnp.zeros((5, 16, 1), traces.dtype)], axis=2)
    picked = jnp.take(padded, slots, axis=2)
    return picked.transpose(2, 0, 1).reshape(3, n_sub, -1)

def residual(field, arrived, ext_index, ext_perm):
    elements = field.shape[2]
    symmetries = symmetry_table()
    traces = face_traces(field)
    incoming = arrived.reshape(-1, 5, 16).transpose(1, 2, 0)
    lookup = jnp.concatenate([traces, incoming, jnp.zeros((5, 16, 1), traces.dtype)], axis=2)
    count = lookup.shape[2]
    flattened = ext_index.reshape(-1).astype(jnp.int32)
    orient = ext_perm.reshape(-1).astype(jnp.int32)
    matches = orient[None, None, :] == jnp.arange(8, dtype=jnp.int32)[:, None, None]
    node_map = lax.optimization_barrier(jnp.sum(jnp.where(matches, jnp.asarray(symmetries)[:, :, None], 0), axis=0)).astype(jnp.int32)
    gather_index = node_map * count + flattened[None, :]
    exterior = jnp.take(lookup.reshape(5, -1), gather_index, axis=1)
    direction = jnp.arange(6 * elements, dtype=jnp.int32) // elements // 2
    component = jnp.arange(5, dtype=jnp.int32)[:, None]
    mirror_sign = jnp.where(component == 1 + direction[None, :], -1.0, 1.0).astype(jnp.float32)[:, None, :]
    at_wall = (flattened == count - 1)[None, None, :]
    exterior = jnp.where(at_wall, traces * mirror_sign, exterior)
    interior = traces.reshape(5, 16, 6, elements)
    exterior = exterior.reshape(5, 16, 6, elements)
    penalty_jump = 0.5 * (normal_flux(interior) - normal_flux(exterior)) + 0.5 * penalty * (exterior - interior)
    jumps = penalty_jump.reshape(5, 4, 4, 6, elements)
    lifted = jnp.zeros((5, 4, 4, 4, elements), jnp.float32)
    lifted = lifted.at[:, 0].add(jumps[:, :, :, 0])
    lifted = lifted.at[:, 3].add(jumps[:, :, :, 1])
    lifted = lifted.at[:, :, 0].add(jumps[:, :, :, 2])
    lifted = lifted.at[:, :, 3].add(jumps[:, :, :, 3])
    lifted = lifted.at[:, :, :, 0].add(jumps[:, :, :, 4])
    lifted = lifted.at[:, :, :, 3].add(jumps[:, :, :, 5])
    return volume_term(field) + lift_factor * lifted.reshape(5, 64, elements)

def global_forward(buffers):
    layout = buffers.reshape(N_DOM, N_SUB, 3, N_SUB, -1)
    groups = []
    for group_id in range(3):
        portion = jnp.roll(layout[:, :, group_id], group_id - 1, axis=0)
        groups.append(jnp.swapaxes(portion, 1, 2))
    return jnp.stack(groups, axis=2).reshape(N_DOM * N_SUB, 3, N_SUB, -1)

def global_backward(gradients):
    layout = gradients.reshape(N_DOM, N_SUB, 3, N_SUB, -1)
    groups = []
    for group_id in range(3):
        portion = jnp.swapaxes(layout[:, :, group_id], 1, 2)
        groups.append(jnp.roll(portion, 1 - group_id, axis=0))
    return jnp.stack(groups, axis=2).reshape(N_DOM * N_SUB, 3, N_SUB, -1)

def reference(state, adjoint_final, send_slot, ext_index, ext_perm):
    devices = N_DOM * N_SUB
    fields = state.reshape(5, 64, devices, E_DEV).transpose(2, 0, 1, 3)
    finals = adjoint_final.reshape(5, 64, devices, E_DEV).transpose(2, 0, 1, 3)
    indices = ext_index.reshape(6, devices, E_DEV).transpose(1, 0, 2)
    orients = ext_perm.reshape(6, devices, E_DEV).transpose(1, 0, 2)

    def evaluate(current):
        outgoing = lax.map(lambda items: pack_sends(items[0], items[1], N_SUB), (current, send_slot))
        rounded = lax.optimization_barrier(outgoing.astype(jnp.bfloat16)).astype(jnp.float32)
        arrived = global_forward(rounded)
        rates = lax.map(lambda items: residual(items[0], items[1], items[2], items[3]), (current, arrived, indices, orients))
        return (rates, arrived)

    def pull_back(current, arrived, cotangent):

        def local_part(items):
            _, pullback = jax.vjp(lambda first, second: residual(first, second, items[3], items[4]), items[0], items[1])
            return pullback(items[2])
        grad_state, grad_arrived = lax.map(local_part, (current, arrived, cotangent, indices, orients))
        returned = global_backward(grad_arrived)

        def pack_part(items):
            _, pullback = jax.vjp(lambda first: pack_sends(first, items[1], N_SUB), items[0])
            return items[2] + pullback(items[3])[0]
        return lax.map(pack_part, (current, send_slot, grad_state, returned))
    rate_first, arrived_first = evaluate(fields)
    middle = fields + step_size * rate_first
    rate_second, arrived_second = evaluate(middle)
    final = 0.5 * fields + 0.5 * (middle + step_size * rate_second)
    back_middle = 0.5 * finals + 0.5 * step_size * pull_back(middle, arrived_second, finals)
    back_start = 0.5 * finals + back_middle + step_size * pull_back(fields, arrived_first, back_middle)
    state_end = final.transpose(1, 2, 0, 3).reshape(5, 64, devices * E_DEV)
    adjoint_start = back_start.transpose(1, 2, 0, 3).reshape(5, 64, devices * E_DEV)
    return (state_end, adjoint_start)
```

```python
import jax
import jax.numpy as jnp
import numpy as np
from jax import lax
from jax.experimental import pallas as pl
from jax.experimental.pallas import tpu as pltpu
from jax.sharding import PartitionSpec as P

step_size = 0.02
mean_flow = 0.3
lift_factor = 12.0
LANES = 128
F32 = jnp.float32
BF16 = jnp.bfloat16


def derivative_table():
    points = np.array([-1.0, -1.0 / np.sqrt(5.0), 1.0 / np.sqrt(5.0), 1.0])
    products = np.array(
        [
            np.prod([points[target] - points[source] for source in range(4) if source != target])
            for target in range(4)
        ]
    )
    result = np.zeros((4, 4))
    for target in range(4):
        for source in range(4):
            if target != source:
                result[target, source] = products[target] / (
                    products[source] * (points[target] - points[source])
                )
        result[target, target] = -np.sum(result[target])
    return result.astype(np.float32)


def constants():
    nodes = np.arange(64).reshape(4, 4, 4)
    select = np.zeros((128, 6 * LANES), np.float32)
    for facet in range(6):
        layer = np.take(nodes, 3 * (facet % 2), axis=facet // 2).reshape(-1)
        for tile in range(3):
            for half in range(2):
                for m in range(16):
                    column = facet * LANES + tile * 32 + half * 16 + m
                    select[half * 64 + layer[m], column] = 1.0
    table = derivative_table()
    eye = np.eye(4, dtype=np.float32)
    along = [
        np.kron(np.kron(table, eye), eye),
        np.kron(np.kron(eye, table), eye),
        np.kron(np.kron(eye, eye), table),
    ]
    pair = np.eye(2, dtype=np.float32)
    forward = np.concatenate([np.kron(pair, -2.0 * d.T) for d in along], axis=0)
    backward = np.concatenate([np.kron(pair, -2.0 * d) for d in along], axis=1)

    def halves(x):
        high = x.astype(jnp.bfloat16)
        return high, (x - high.astype(np.float32)).astype(jnp.bfloat16)

    return (select.astype(jnp.bfloat16), select.T.astype(jnp.bfloat16), *halves(forward), *halves(backward))


def halves(x):
    high = x.astype(BF16)
    return high, (x - high.astype(F32)).astype(BF16)


def dot(x, y):
    return jnp.dot(x, y, preferred_element_type=F32)


def dot_split(x, w):
    high, low = halves(x)
    both = dot(jnp.concatenate([high, low], axis=0), w)
    return both[: x.shape[0]] + both[x.shape[0] :]


def dot_full(x, w_high, w_low):
    high, low = halves(x)
    both = dot(jnp.concatenate([high, low], axis=0), w_high)
    return both[: x.shape[0]] + both[x.shape[0] :] + dot(high, w_low)


def lanes_of(x, index):
    return jnp.take_along_axis(x, index, axis=1, mode="promise_in_bounds")


def iota(shape, axis):
    return lax.broadcasted_iota(jnp.int32, shape, axis)


def to_rows(x, elements):
    flat = x.reshape(320, elements)
    flat = jnp.concatenate([flat, jnp.zeros((64, elements), F32)], axis=0)
    return jnp.concatenate([flat[LANES * t : LANES * (t + 1)].T for t in range(3)], axis=0)


def from_rows(x, elements):
    return [x[elements * t : elements * (t + 1)].T for t in range(3)]


def traces(x, select, elements):
    wide = dot_split(x, select)
    block = iota((elements, LANES), 1) // 32
    parts = []
    for facet in range(6):
        cut = wide[:, LANES * facet : LANES * (facet + 1)]
        a, b, c = (cut[elements * t : elements * (t + 1)] for t in range(3))
        parts.append(jnp.where(block == 0, a, jnp.where(block == 1, b, c)))
    return jnp.concatenate(parts, axis=0)


def lift(x, select_t, elements):
    block = iota((elements, LANES), 1) // 32
    rows = []
    for t in range(3):
        rows.append(
            jnp.concatenate(
                [
                    jnp.where(block == t, x[elements * f : elements * (f + 1)], 0.0)
                    for f in range(6)
                ],
                axis=1,
            )
        )
    return dot_split(jnp.concatenate(rows, axis=0), select_t)


def volume_tables(elements):
    shape = (3 * elements, LANES)
    member = 2 * (iota(shape, 0) // elements) + iota(shape, 1) // 64
    return member


def spread(x, var, elements):
    tile, half = var // 2, var % 2
    part = x[elements * tile : elements * (tile + 1)]
    other = pltpu.roll(part, 64, 1)
    both = jnp.where(iota(part.shape, 1) // 64 == half, part, other)
    return jnp.concatenate([both] * 3, axis=0)


def volume(x, d_high, d_low, elements):
    member = volume_tables(elements)
    ends = jnp.where((member == 0) | (member == 4), 1.0, 0.0)
    pressure = spread(x, 4, elements)
    fluxes = []
    for a in range(3):
        speed = spread(x, 1 + a, elements)
        drift = mean_flow if a == 0 else 0.0
        fluxes.append(
            x * (speed + drift) + ends * speed + jnp.where(member == 1 + a, pressure, 0.0)
        )
    return dot_full(jnp.concatenate(fluxes, axis=1), d_high, d_low)


def volume_back(x, slopes, elements):
    member = volume_tables(elements)
    ends = jnp.where((member == 0) | (member == 4), 1.0, 0.0)
    total = None
    for a in range(3):
        g = slopes[:, LANES * a : LANES * (a + 1)]
        drift = mean_flow if a == 0 else 0.0
        speed = spread(x, 1 + a, elements)
        product = (x + ends) * g
        summed = product[:elements] + product[elements : 2 * elements] + product[2 * elements :]
        summed = summed + pltpu.roll(summed, 64, 1)
        summed = jnp.concatenate([summed] * 3, axis=0)
        term = (speed + drift) * g + jnp.where(member == 1 + a, summed, 0.0)
        term = term + jnp.where(member == 4, spread(g, 1 + a, elements), 0.0)
        total = term if total is None else total + term
    return total


class Faces:
    def __init__(self, elements):
        shape = (6 * elements, LANES)
        lane = iota(shape, 1)
        facet = iota(shape, 0) // elements
        self.node = lane % 16
        self.member = lane // 16
        self.axis = facet // 2
        self.sign = (2 * (facet % 2) - 1).astype(F32)
        self.drift = jnp.where(self.axis == 0, mean_flow, 0.0)
        self.normal = self.member == 1 + self.axis
        self.ends = jnp.where((self.member == 0) | (self.member == 4), 1.0, 0.0)
        self.mirror = jnp.where(self.normal, -1.0, 1.0)
        self.at_speed = (1 + self.axis) * 16 + self.node
        self.at_pressure = 64 + self.node

    def flux(self, q):
        speed = lanes_of(q, self.at_speed)
        pressure = lanes_of(q, self.at_pressure)
        return self.sign * (
            q * (speed + self.drift) + self.ends * speed + jnp.where(self.normal, pressure, 0.0)
        )

    def back(self, q, w, axis=None):
        if axis is None:
            at, drift, normal = self.at_speed, self.drift, self.normal
        else:
            at = (1 + axis) * 16 + self.node
            drift = mean_flow if axis == 0 else 0.0
            normal = self.member == 1 + axis
        product = (q + self.ends) * w
        for shift in (64, 32, 16):
            product = product + pltpu.roll(product, shift, 1)
        term = (lanes_of(q, at) + drift) * w + jnp.where(normal, product, 0.0)
        return term + jnp.where(self.member == 4, lanes_of(w, at), 0.0)

    def jump(self, inner, outer):
        return 0.5 * (self.flux(inner) - self.flux(outer)) + (outer - inner)


def column(values, elements):
    lead, width = values.shape
    x = values.astype(F32)
    x = jnp.concatenate([x, jnp.zeros((8 - lead, width), F32)], axis=0)
    x = x.T
    return jnp.concatenate([x[:, f : f + 1] for f in range(lead)], axis=0).astype(jnp.int32)


def one_hot(flags):
    return jnp.where(flags, 1.0, 0.0).astype(BF16)


def program(state, final, slots, ext_row, ext, perm, mats, net):
    select, select_t, d_high, d_low, b_high, b_low = (m[...] for m in mats)
    elements = state.shape[2]
    n_faces = 6 * elements
    n_slots = slots.shape[1]
    faces = Faces(elements)

    net.greet()
    x0 = to_rows(state, elements)
    t0 = traces(x0, select, elements)
    slot_column = column(slots, elements)
    pick = one_hot(slot_column == iota((n_slots, n_faces), 1))
    net.send(0, lambda: dot(pick, t0.astype(BF16)).astype(BF16))

    ext_column = column(ext, elements)
    perm_column = column(perm, elements) + jnp.zeros((n_faces, LANES), jnp.int32)
    wall = ext_column + jnp.zeros((n_faces, LANES), jnp.int32) == n_faces + n_slots
    flip_r = (perm_column & 1) != 0
    flip_s = (perm_column & 2) != 0
    swap = (perm_column & 4) != 0
    base = faces.member * 16
    r, s = faces.node // 4, faces.node % 4
    r_new = jnp.where(flip_r, 3 - r, r)
    s_new = jnp.where(flip_s, 3 - s, s)
    orient = base + jnp.where(swap, 4 * s_new + r_new, 4 * r_new + s_new)
    r_old = jnp.where(swap, s, r)
    s_old = jnp.where(swap, r, s)
    r_old = jnp.where(flip_r, 3 - r_old, r_old)
    s_old = jnp.where(flip_s, 3 - s_old, s_old)
    unorient = base + 4 * r_old + s_old

    to_local = one_hot(ext_row == iota((n_faces, n_faces), 0))
    to_slots = one_hot(ext_row - n_faces == iota((n_slots, n_faces), 0))
    unpick = one_hot(slots == iota((n_faces, n_slots), 0))

    w = to_rows(final, elements)
    w_jump = lift_factor * traces(w, select, elements)
    w_turned = lanes_of(jnp.where(wall, 0.0, w_jump), unorient)

    def by_axis(x):
        signed = faces.sign * x
        return jnp.concatenate(
            [jnp.where(faces.axis == a, signed, 0.0) for a in range(3)] + [x], axis=1
        )

    cot = by_axis(w_turned)
    cot_high, cot_low = halves(cot)
    net.send(1, lambda: dot(to_slots, cot_high).astype(BF16))

    from_local = one_hot(ext_column == iota((n_faces, n_faces), 1))
    from_slots = one_hot(ext_column - n_faces == iota((n_faces, n_slots), 1))

    def outer_local(t):
        both = dot(from_local, jnp.concatenate(halves(t), axis=1))
        return both[:, :LANES] + both[:, LANES:]

    def outer(t, local, received):
        e = lanes_of(local + dot(from_slots, received), orient)
        return jnp.where(wall, t * faces.mirror, e)

    def jump(t, e):
        return faces.jump(t, e)

    local0 = outer_local(t0)
    rate0 = volume(x0, d_high, d_low, elements)
    cot_local = dot(to_local, cot_high) + dot(to_local, cot_low) - by_axis(w_jump)
    slopes = dot_full(w, b_high, b_low)

    e0 = outer(t0, local0, net.wait(0))
    x1 = x0 + step_size * (rate0 + lift_factor * lift(jump(t0, e0), select_t, elements))
    t1 = traces(x1, select, elements)
    net.send(2, lambda: dot(pick, t1.astype(BF16)).astype(BF16))

    back1 = volume_back(x1, slopes, elements)
    wall_out = w_jump - 0.5 * faces.sign * faces.back(t1 * faces.mirror, w_jump)
    t_bar = jnp.where(wall, faces.mirror * wall_out, 0.0)
    cot_all = cot_local + dot(unpick, net.wait(1))
    t_bar = t_bar + cot_all[:, 3 * LANES :]
    for a in range(3):
        t_bar = t_bar - 0.5 * faces.back(t1, cot_all[:, LANES * a : LANES * (a + 1)], a)
    w1 = 0.5 * w + 0.5 * step_size * (back1 + lift(t_bar, select_t, elements))

    w1_jump = lift_factor * traces(w1, select, elements)
    out_bar = w1_jump - 0.5 * faces.sign * faces.back(e0, w1_jump)
    turned = lanes_of(jnp.where(wall, 0.0, out_bar), unorient)
    turned_high, turned_low = halves(turned)
    net.send(3, lambda: dot(to_slots, turned_high).astype(BF16))

    in_bar = 0.5 * faces.sign * faces.back(t0, w1_jump) - w1_jump
    in_bar = in_bar + jnp.where(wall, faces.mirror * out_bar, 0.0)
    in_bar = in_bar + dot(to_local, turned_high) + dot(to_local, turned_low)
    slopes1 = dot_full(w1, b_high, b_low)
    back0 = volume_back(x0, slopes1, elements)
    start = 0.5 * w + w1 + step_size * back0

    local1 = outer_local(t1)
    rate1 = volume(x1, d_high, d_low, elements)
    e1 = outer(t1, local1, net.wait(2))
    rate1 = rate1 + lift_factor * lift(jump(t1, e1), select_t, elements)
    net.output(0, from_rows(0.5 * x0 + 0.5 * (x1 + step_size * rate1), elements))

    in_bar = in_bar + dot(unpick, net.wait(3))
    start = start + step_size * lift(in_bar, select_t, elements)
    net.output(1, from_rows(start, elements))


class Net:
    def __init__(self, n_dom, n_sub, outs, send_bufs, recv_bufs, send_sem, recv_sem):
        self.n_dom, self.n_sub = n_dom, n_sub
        self.dom, self.sub = lax.axis_index("dom"), lax.axis_index("sub")
        self.outs = outs
        self.send_bufs, self.recv_bufs = send_bufs, recv_bufs
        self.send_sem, self.recv_sem = send_sem, recv_sem
        self.greeted = False

    def partners(self):
        for group in (0, 2, 1):
            for j in range(self.n_sub):
                if group != 1 or j != 0:
                    yield group, lax.rem(self.sub + j, self.n_sub)

    def neighbour(self, steps):
        return lax.rem(self.dom + steps + self.n_dom, self.n_dom)

    def greet(self):
        barrier = pltpu.get_barrier_semaphore()
        for group, other in self.partners():
            pl.semaphore_signal(
                barrier,
                inc=1,
                device_id=(self.neighbour(group - 1), other),
                device_id_type=pl.DeviceIdType.MESH,
            )

    def copies(self, phase):
        source, target = self.send_bufs[phase], self.recv_bufs[phase]
        size = source.shape[0] // (3 * self.n_sub)
        way = 1 if phase % 2 == 0 else -1
        for group, other in self.partners():
            there = pl.multiple_of((group * self.n_sub + other) * size, size)
            here = pl.multiple_of((group * self.n_sub + self.sub) * size, size)
            yield pltpu.make_async_remote_copy(
                src_ref=source.at[pl.ds(there, size)],
                dst_ref=target.at[pl.ds(here, size)],
                send_sem=self.send_sem.at[phase, group * self.n_sub + other],
                recv_sem=self.recv_sem.at[phase, group * self.n_sub + self.sub],
                device_id=(self.neighbour(way * (group - 1)), other),
                device_id_type=pl.DeviceIdType.MESH,
            )

    def send(self, phase, make):
        source, target = self.send_bufs[phase], self.recv_bufs[phase]
        source[...] = make()
        if not self.greeted:
            pl.semaphore_wait(pltpu.get_barrier_semaphore(), 3 * self.n_sub - 1)
            self.greeted = True
        for copy in self.copies(phase):
            copy.start()
        size = source.shape[0] // (3 * self.n_sub)
        own = pl.ds(pl.multiple_of((self.n_sub + self.sub) * size, size), size)
        target[own] = source[own]

    def wait(self, phase):
        source, target = self.send_bufs[phase], self.recv_bufs[phase]
        size = source.shape[0] // (3 * self.n_sub)
        for group, other in self.partners():
            rows = pl.ds(pl.multiple_of((group * self.n_sub + other) * size, size), size)
            index = group * self.n_sub + other
            pltpu.make_async_remote_copy(
                src_ref=source.at[rows],
                dst_ref=target.at[rows],
                send_sem=self.send_sem.at[phase, index],
                recv_sem=self.recv_sem.at[phase, index],
                device_id=(self.neighbour(group - 1), other),
                device_id_type=pl.DeviceIdType.MESH,
            ).wait_recv()
        return target[...]

    def finish(self):
        for phase in range(4):
            for copy in self.copies(phase):
                copy.wait_send()

    def output(self, which, parts):
        for t in range(3):
            for half in range(2):
                if 2 * t + half < 5:
                    self.outs[which][2 * t + half] = parts[t][64 * half : 64 * (half + 1)]


def kernel(n_dom, n_sub, *refs):
    state, final, slots, ext_row, ext, perm = refs[:6]
    mats = refs[6:12]
    outs = refs[12:14]
    send_bufs, recv_bufs = refs[14:18], refs[18:22]
    net = Net(n_dom, n_sub, outs, send_bufs, recv_bufs, refs[22], refs[23])
    program(state[...], final[...], slots[...], ext_row[...], ext[...], perm[...], mats, net)
    net.finish()


def solution(mesh):
    n_dom, n_sub = mesh.shape["dom"], mesh.shape["sub"]
    mats = constants()

    def shards(state, final, send_slot, ext_index, ext_perm):
        n_slots = send_slot.shape[1]
        widths = (LANES, 4 * LANES, LANES, LANES)
        vmem = pl.BlockSpec(memory_space=pltpu.VMEM)
        buffers = [pltpu.VMEM((n_slots, width), BF16) for width in widths]
        result = jax.ShapeDtypeStruct(state.shape, F32)
        return pl.pallas_call(
            lambda *refs: kernel(n_dom, n_sub, *refs),
            out_shape=(result, result),
            in_specs=[vmem] * 12,
            out_specs=(vmem, vmem),
            scratch_shapes=buffers
            + buffers
            + [
                pltpu.SemaphoreType.DMA((4, 3 * n_sub)),
                pltpu.SemaphoreType.DMA((4, 3 * n_sub)),
            ],
            compiler_params=pltpu.CompilerParams(
                collective_id=0, has_side_effects=True, vmem_limit_bytes=32 * 1024 * 1024
            ),
        )(
            state,
            final,
            send_slot,
            ext_index.reshape(1, -1),
            ext_index,
            ext_perm,
            *[jnp.asarray(m) for m in mats],
        )

    return jax.shard_map(
        shards,
        mesh=mesh,
        in_specs=(
            P(None, None, ("dom", "sub")),
            P(None, None, ("dom", "sub")),
            P(("dom", "sub"), None),
            P(None, ("dom", "sub")),
            P(None, ("dom", "sub")),
        ),
        out_specs=(P(None, None, ("dom", "sub")), P(None, None, ("dom", "sub"))),
        check_vma=False,
    )
```

```python
import jax
import jax.numpy as jnp
import numpy as np
from jax import lax
from jax.experimental import pallas as pl
from jax.experimental.pallas import tpu as pltpu
from jax.sharding import PartitionSpec as P

step_size = 0.02
mean_flow = 0.3
lift_factor = 12.0
LANES = 128
F32 = jnp.float32
BF16 = jnp.bfloat16


def derivative_table():
    points = np.array([-1.0, -1.0 / np.sqrt(5.0), 1.0 / np.sqrt(5.0), 1.0])
    products = np.array(
        [
            np.prod([points[target] - points[source] for source in range(4) if source != target])
            for target in range(4)
        ]
    )
    result = np.zeros((4, 4))
    for target in range(4):
        for source in range(4):
            if target != source:
                result[target, source] = products[target] / (
                    products[source] * (points[target] - points[source])
                )
        result[target, target] = -np.sum(result[target])
    return result.astype(np.float32)


def constants():
    table = derivative_table()
    eye = np.eye(4, dtype=np.float32)
    along = [
        np.kron(np.kron(table, eye), eye),
        np.kron(np.kron(eye, table), eye),
        np.kron(np.kron(eye, eye), table),
    ]
    pair = np.eye(2, dtype=np.float32)
    parts = []
    for d in ([x.T for x in along], along):
        full = np.concatenate([np.kron(pair, -2.0 * x) for x in d], axis=0)
        high = full.astype(jnp.bfloat16)
        parts += [high, (full - high.astype(np.float32)).astype(jnp.bfloat16)]
    return np.concatenate(parts, axis=0)


def halves(x):
    high = x.astype(BF16)
    return high, (x - high.astype(F32)).astype(BF16)


def dot(x, y):
    return jnp.dot(x, y, preferred_element_type=F32)


def dot_full(x, w_high, w_low):
    high, low = halves(x)
    both = dot(jnp.concatenate([high, low], axis=0), w_high)
    return both[: x.shape[0]] + both[x.shape[0] :] + dot(high, w_low)


def lanes_of(x, index):
    return jnp.take_along_axis(x, index, axis=1, mode="promise_in_bounds")


def iota(shape, axis):
    return lax.broadcasted_iota(jnp.int32, shape, axis)


def dot_stacked(x, w_high, w_low):
    high, low = halves(x)
    wide = jnp.concatenate(
        [
            jnp.concatenate([high, high], axis=1),
            jnp.concatenate([low, jnp.zeros_like(low)], axis=1),
        ],
        axis=0,
    )
    both = dot(wide, jnp.concatenate([w_high, w_low], axis=0))
    return both[: x.shape[0]] + both[x.shape[0] :]


def to_rows(x):
    pairs = [jnp.concatenate([x[2 * t], x[2 * t + 1]], axis=1) for t in range(2)]
    pairs.append(jnp.concatenate([x[4], jnp.zeros_like(x[4])], axis=1))
    return jnp.concatenate(pairs, axis=0)


def traces(x, elements):
    lane = iota((elements, LANES), 1)
    block = lane // 32
    m = lane % 16
    parts = []
    for facet in range(6):
        layer = 3 * (facet % 2)
        if facet < 2:
            node = 16 * layer + m
        elif facet < 4:
            node = 16 * (m // 4) + 4 * layer + m % 4
        else:
            node = 4 * m + layer
        at = jnp.where(block == 3, 64, 64 * (lane // 16 % 2) + node)
        a, b, c = (lanes_of(x[elements * t : elements * (t + 1)], at) for t in range(3))
        parts.append(jnp.where(block == 0, a, jnp.where(block == 1, b, c)))
    return jnp.concatenate(parts, axis=0)


def lift(x, elements):
    lane = iota((elements, LANES), 1)
    half, node = lane // 64, lane % 64
    i, j, k = node // 16, node // 4 % 4, node % 4
    rows = []
    for t in range(3):
        base = (2 * t + half) * 16
        total = None
        for axis, (along, m) in enumerate(((i, node % 16), (j, 4 * i + k), (k, 4 * i + j))):
            low, high = (
                lanes_of(x[elements * f : elements * (f + 1)], base + m)
                for f in (2 * axis, 2 * axis + 1)
            )
            term = jnp.where(along == 0, low, jnp.where(along == 3, high, 0.0))
            total = term if total is None else total + term
        rows.append(total)
    return jnp.concatenate(rows, axis=0)


def volume_tables(elements):
    shape = (3 * elements, LANES)
    member = 2 * (iota(shape, 0) // elements) + iota(shape, 1) // 64
    return member


def spread(x, var, elements):
    tile, half = var // 2, var % 2
    part = x[elements * tile : elements * (tile + 1)]
    other = pltpu.roll(part, 64, 1)
    both = jnp.where(iota(part.shape, 1) // 64 == half, part, other)
    return jnp.concatenate([both] * 3, axis=0)


def volume(x, d_high, d_low, elements):
    member = volume_tables(elements)
    ends = jnp.where((member == 0) | (member == 4), 1.0, 0.0)
    pressure = spread(x, 4, elements)
    fluxes = []
    for a in range(3):
        speed = spread(x, 1 + a, elements)
        drift = mean_flow if a == 0 else 0.0
        fluxes.append(
            x * (speed + drift) + ends * speed + jnp.where(member == 1 + a, pressure, 0.0)
        )
    return dot_full(jnp.concatenate(fluxes, axis=1), d_high, d_low)


def volume_back(x, slopes, elements):
    member = volume_tables(elements)
    ends = jnp.where((member == 0) | (member == 4), 1.0, 0.0)
    total = None
    for a in range(3):
        g = slopes[:, LANES * a : LANES * (a + 1)]
        drift = mean_flow if a == 0 else 0.0
        speed = spread(x, 1 + a, elements)
        product = (x + ends) * g
        summed = product[:elements] + product[elements : 2 * elements] + product[2 * elements :]
        summed = summed + pltpu.roll(summed, 64, 1)
        summed = jnp.concatenate([summed] * 3, axis=0)
        term = (speed + drift) * g + jnp.where(member == 1 + a, summed, 0.0)
        term = term + jnp.where(member == 4, spread(g, 1 + a, elements), 0.0)
        total = term if total is None else total + term
    return total


class Faces:
    def __init__(self, elements):
        shape = (6 * elements, LANES)
        lane = iota(shape, 1)
        facet = iota(shape, 0) // elements
        self.node = lane % 16
        self.member = lane // 16
        self.axis = facet // 2
        self.sign = (2 * (facet % 2) - 1).astype(F32)
        self.drift = jnp.where(self.axis == 0, mean_flow, 0.0)
        self.normal = self.member == 1 + self.axis
        self.ends = jnp.where((self.member == 0) | (self.member == 4), 1.0, 0.0)
        self.mirror = jnp.where(self.normal, -1.0, 1.0)
        self.at_speed = (1 + self.axis) * 16 + self.node
        self.at_pressure = 64 + self.node

    def flux(self, q):
        speed = lanes_of(q, self.at_speed)
        pressure = lanes_of(q, self.at_pressure)
        return self.sign * (
            q * (speed + self.drift) + self.ends * speed + jnp.where(self.normal, pressure, 0.0)
        )

    def back(self, q, w, axis=None):
        if axis is None:
            at, drift, normal = self.at_speed, self.drift, self.normal
        else:
            at = (1 + axis) * 16 + self.node
            drift = mean_flow if axis == 0 else 0.0
            normal = self.member == 1 + axis
        product = (q + self.ends) * w
        for shift in (64, 32, 16):
            product = product + pltpu.roll(product, shift, 1)
        term = (lanes_of(q, at) + drift) * w + jnp.where(normal, product, 0.0)
        return term + jnp.where(self.member == 4, lanes_of(w, at), 0.0)

    def jump(self, inner, outer):
        return 0.5 * (self.flux(inner) - self.flux(outer)) + (outer - inner)


def column(values):
    lead, width = values.shape
    x = values.astype(F32)
    x = jnp.concatenate([x, jnp.zeros((8 - lead, width), F32)], axis=0)
    x = x.T
    return jnp.concatenate([x[:, f : f + 1] for f in range(lead)], axis=0).astype(jnp.int32)


def one_hot(flags):
    return jnp.where(flags, 1.0, 0.0).astype(BF16)


def program(net):
    net.greet()
    state = net.load(0)
    elements = state.shape[1]
    n_faces = 6 * elements
    faces = Faces(elements)
    x0 = to_rows(state)
    t0 = traces(x0, elements)
    slots = net.load(1)
    n_slots = slots.shape[1]
    slot_column = column(slots)
    pick = one_hot(slot_column == iota((n_slots, n_faces), 1))
    net.send(0, lambda: dot(pick, t0.astype(BF16)).astype(BF16))

    ext = net.load(2)
    ext_row = jnp.concatenate([ext[f : f + 1] for f in range(6)], axis=1)
    ext_column = column(ext)
    perm_column = column(net.load(3)) + jnp.zeros((n_faces, LANES), jnp.int32)
    wall = ext_column + jnp.zeros((n_faces, LANES), jnp.int32) == n_faces + n_slots
    flip_r = (perm_column & 1) != 0
    flip_s = (perm_column & 2) != 0
    swap = (perm_column & 4) != 0
    base = faces.member * 16
    r, s = faces.node // 4, faces.node % 4
    r_new = jnp.where(flip_r, 3 - r, r)
    s_new = jnp.where(flip_s, 3 - s, s)
    orient = base + jnp.where(swap, 4 * s_new + r_new, 4 * r_new + s_new)
    r_old = jnp.where(swap, s, r)
    s_old = jnp.where(swap, r, s)
    r_old = jnp.where(flip_r, 3 - r_old, r_old)
    s_old = jnp.where(flip_s, 3 - s_old, s_old)
    unorient = base + 4 * r_old + s_old

    to_local = one_hot(ext_row == iota((n_faces, n_faces), 0))
    to_slots = one_hot(ext_row - n_faces == iota((n_slots, n_faces), 0))
    unpick = one_hot(slots == iota((n_faces, n_slots), 0))

    w = to_rows(net.load(4))
    w_jump = lift_factor * traces(w, elements)
    w_turned = lanes_of(jnp.where(wall, 0.0, w_jump), unorient)

    spare = faces.member >= 5

    def by_axis(x):
        signed = faces.sign * x
        tiles = [jnp.where(faces.axis == a, signed, 0.0) for a in range(3)]
        tiles[0] = jnp.where(spare, pltpu.roll(x, 80, 1), tiles[0])
        tiles[1] = jnp.where(spare, pltpu.roll(x, 32, 1), tiles[1])
        return jnp.concatenate(tiles, axis=1)

    def unpacked(x):
        tiles = [x[:, LANES * a : LANES * (a + 1)] for a in range(3)]
        plain = jnp.where(
            faces.member < 3,
            pltpu.roll(tiles[0], 48, 1),
            jnp.where(spare, 0.0, pltpu.roll(tiles[1], 96, 1)),
        )
        return [jnp.where(spare, 0.0, tiles[0]), jnp.where(spare, 0.0, tiles[1]), tiles[2], plain]

    cot_high, cot_low = halves(by_axis(w_turned))
    net.send(1, lambda: dot(to_slots, cot_high).astype(BF16))

    from_local = one_hot(ext_column == iota((n_faces, n_faces), 1))
    from_slots = one_hot(ext_column - n_faces == iota((n_faces, n_slots), 1))

    def outer_local(t):
        both = dot(from_local, jnp.concatenate(halves(t), axis=1))
        return both[:, :LANES] + both[:, LANES:]

    def outer(t, local, received):
        e = lanes_of(local + dot(from_slots, received), orient)
        return jnp.where(wall, t * faces.mirror, e)

    def jump(t, e):
        return faces.jump(t, e)

    local0 = outer_local(t0)
    size = 3 * LANES
    mats = net.load(5)
    d_high, d_low = mats[:size], mats[size : 2 * size]
    b_high, b_low = (
        jnp.concatenate([mats[at + LANES * a : at + LANES * (a + 1)] for a in range(3)], axis=1)
        for at in (2 * size, 3 * size)
    )
    rate0 = volume(x0, d_high, d_low, elements)
    cot_local = dot(to_local, cot_high) + dot(to_local, cot_low) - by_axis(w_jump)
    slopes = dot_stacked(w, b_high, b_low)

    e0 = outer(t0, local0, net.wait(0))
    x1 = x0 + step_size * (rate0 + lift_factor * lift(jump(t0, e0), elements))
    t1 = traces(x1, elements)
    net.send(2, lambda: dot(pick, t1.astype(BF16)).astype(BF16))

    back1 = volume_back(x1, slopes, elements)
    wall_out = w_jump - 0.5 * faces.sign * faces.back(t1 * faces.mirror, w_jump)
    t_bar = jnp.where(wall, faces.mirror * wall_out, 0.0)
    cot_all = unpacked(cot_local + dot(unpick, net.wait(1)))
    t_bar = t_bar + cot_all[3]
    for a in range(3):
        t_bar = t_bar - 0.5 * faces.back(t1, cot_all[a], a)
    w1 = 0.5 * w + 0.5 * step_size * (back1 + lift(t_bar, elements))

    w1_jump = lift_factor * traces(w1, elements)
    out_bar = w1_jump - 0.5 * faces.sign * faces.back(e0, w1_jump)
    turned = lanes_of(jnp.where(wall, 0.0, out_bar), unorient)
    turned_high, turned_low = halves(turned)
    net.send(3, lambda: dot(to_slots, turned_high).astype(BF16))

    in_bar = 0.5 * faces.sign * faces.back(t0, w1_jump) - w1_jump
    in_bar = in_bar + jnp.where(wall, faces.mirror * out_bar, 0.0)
    in_bar = in_bar + dot(to_local, turned_high) + dot(to_local, turned_low)
    slopes1 = dot_stacked(w1, b_high, b_low)
    back0 = volume_back(x0, slopes1, elements)
    start = w1 - 0.5 * w + step_size * back0

    local1 = outer_local(t1)
    rate1 = volume(x1, d_high, d_low, elements)
    e1 = outer(t1, local1, net.wait(2))
    rate1 = rate1 + lift_factor * lift(jump(t1, e1), elements)
    net.output(0, 0.5 * (x1 - x0) + 0.5 * step_size * rate1)

    in_bar = in_bar + dot(unpick, net.wait(3))
    start = start + step_size * lift(in_bar, elements)
    net.output(1, start)


class Net:
    def __init__(
        self, n_dom, n_sub, inputs, held, send_bufs, recv_bufs, send_sem, recv_sem, load_sem
    ):
        self.n_dom, self.n_sub = n_dom, n_sub
        self.dom, self.sub = lax.axis_index("dom"), lax.axis_index("sub")
        self.send_bufs, self.recv_bufs = send_bufs, recv_bufs
        self.send_sem, self.recv_sem = send_sem, recv_sem
        self.greeted = False
        self.held = held
        self.loads = [
            pltpu.make_async_copy(inputs[n], held[n], load_sem.at[n]) for n in range(len(held))
        ]
        for load in self.loads:
            load.start()

    def load(self, which):
        self.loads[which].wait()
        return self.held[which][...]

    def partners(self):
        for group in (0, 2, 1):
            for j in range(self.n_sub):
                if group != 1 or j != 0:
                    yield group, lax.rem(self.sub + j, self.n_sub)

    def neighbour(self, steps):
        return lax.rem(self.dom + steps + self.n_dom, self.n_dom)

    def greet(self):
        barrier = pltpu.get_barrier_semaphore()
        for group, other in self.partners():
            pl.semaphore_signal(
                barrier,
                inc=1,
                device_id=(self.neighbour(group - 1), other),
                device_id_type=pl.DeviceIdType.MESH,
            )

    def copies(self, phase):
        source, target = self.send_bufs[phase], self.recv_bufs[phase]
        size = source.shape[0] // (3 * self.n_sub)
        way = 1 if phase % 2 == 0 else -1
        for group, other in self.partners():
            there = pl.multiple_of((group * self.n_sub + other) * size, size)
            here = pl.multiple_of((group * self.n_sub + self.sub) * size, size)
            yield pltpu.make_async_remote_copy(
                src_ref=source.at[pl.ds(there, size)],
                dst_ref=target.at[pl.ds(here, size)],
                send_sem=self.send_sem.at[phase, group * self.n_sub + other],
                recv_sem=self.recv_sem.at[phase, group * self.n_sub + self.sub],
                device_id=(self.neighbour(way * (group - 1)), other),
                device_id_type=pl.DeviceIdType.MESH,
            )

    def send(self, phase, make):
        source, target = self.send_bufs[phase], self.recv_bufs[phase]
        source[...] = make()
        if not self.greeted:
            pl.semaphore_wait(pltpu.get_barrier_semaphore(), 3 * self.n_sub - 1)
            self.greeted = True
        for copy in self.copies(phase):
            copy.start()
        size = source.shape[0] // (3 * self.n_sub)
        own = pl.ds(pl.multiple_of((self.n_sub + self.sub) * size, size), size)
        target[own] = source[own]

    def wait(self, phase):
        source, target = self.send_bufs[phase], self.recv_bufs[phase]
        size = source.shape[0] // (3 * self.n_sub)
        for group, other in self.partners():
            rows = pl.ds(pl.multiple_of((group * self.n_sub + other) * size, size), size)
            index = group * self.n_sub + other
            pltpu.make_async_remote_copy(
                src_ref=source.at[rows],
                dst_ref=target.at[rows],
                send_sem=self.send_sem.at[phase, index],
                recv_sem=self.recv_sem.at[phase, index],
                device_id=(self.neighbour(group - 1), other),
                device_id_type=pl.DeviceIdType.MESH,
            ).wait_recv()
        return target[...]

    def finish(self):
        for phase in range(4):
            for copy in self.copies(phase):
                copy.wait_send()
        for store in self.stores:
            store.wait()

    def output(self, which, x):
        elements = x.shape[0] // 3
        for member in range(5):
            tile, half = member // 2, member % 2
            self.staged[5 * which + member] = x[
                elements * tile : elements * (tile + 1), 64 * half : 64 * (half + 1)
            ]
        self.stores[which].start()


def kernel(n_dom, n_sub, *refs):
    inputs, out, held, staged = refs[:6], refs[6], refs[7:13], refs[13]
    send_bufs, recv_bufs = refs[14:18], refs[18:22]
    send_sem, recv_sem, load_sem, store_sem = refs[22:]
    net = Net(n_dom, n_sub, inputs, held, send_bufs, recv_bufs, send_sem, recv_sem, load_sem)
    net.staged = staged
    net.stores = [
        pltpu.make_async_copy(
            staged.at[pl.ds(5 * n, 5)], out.at[pl.ds(5 * n, 5)], store_sem.at[n]
        )
        for n in range(2)
    ]
    program(net)
    net.finish()


def solution(mesh):
    n_dom, n_sub = mesh.shape["dom"], mesh.shape["sub"]
    mats = constants()

    def shards(state, final, send_slot, ext_index, ext_perm):
        n_slots = send_slot.shape[1]
        widths = (LANES, 3 * LANES, LANES, LANES)
        buffers = [pltpu.VMEM((n_slots, width), BF16) for width in widths]
        operands = [
            state.transpose(0, 2, 1),
            send_slot,
            ext_index,
            ext_perm,
            final.transpose(0, 2, 1),
            jnp.asarray(mats),
        ]
        elements = state.shape[2]
        result = jax.ShapeDtypeStruct((10, elements, 64), F32)
        hbm = pl.BlockSpec(memory_space=pltpu.HBM)
        change = pl.pallas_call(
            lambda *refs: kernel(n_dom, n_sub, *refs),
            out_shape=result,
            in_specs=[hbm] * 6,
            out_specs=hbm,
            scratch_shapes=[pltpu.VMEM(x.shape, x.dtype) for x in operands]
            + [pltpu.VMEM((10, elements, 64), F32)]
            + buffers
            + buffers
            + [
                pltpu.SemaphoreType.DMA((4, 3 * n_sub)),
                pltpu.SemaphoreType.DMA((4, 3 * n_sub)),
                pltpu.SemaphoreType.DMA((6,)),
                pltpu.SemaphoreType.DMA((2,)),
            ],
            compiler_params=pltpu.CompilerParams(
                collective_id=0, has_side_effects=True, vmem_limit_bytes=60 * 1024 * 1024
            ),
        )(*operands)
        change = change.transpose(0, 2, 1)
        return state + change[:5], final + change[5:]

    return jax.shard_map(
        shards,
        mesh=mesh,
        in_specs=(
            P(None, None, ("dom", "sub")),
            P(None, None, ("dom", "sub")),
            P(("dom", "sub"), None),
            P(None, ("dom", "sub")),
            P(None, ("dom", "sub")),
        ),
        out_specs=(P(None, None, ("dom", "sub")), P(None, None, ("dom", "sub"))),
        check_vma=False,
    )
```

```python
import jax
import jax.numpy as jnp
import numpy as np
from jax import lax
from jax.experimental import pallas as pl
from jax.experimental.pallas import tpu as pltpu
from jax.sharding import PartitionSpec as P

step_size = 0.02
mean_flow = 0.3
lift_factor = 12.0
LANES = 128
F32 = jnp.float32
BF16 = jnp.bfloat16


def derivative_table():
    points = np.array([-1.0, -1.0 / np.sqrt(5.0), 1.0 / np.sqrt(5.0), 1.0])
    products = np.array(
        [
            np.prod([points[target] - points[source] for source in range(4) if source != target])
            for target in range(4)
        ]
    )
    result = np.zeros((4, 4))
    for target in range(4):
        for source in range(4):
            if target != source:
                result[target, source] = products[target] / (
                    products[source] * (points[target] - points[source])
                )
        result[target, target] = -np.sum(result[target])
    return result.astype(np.float32)


def constants():
    table = derivative_table()
    eye = np.eye(4, dtype=np.float32)
    along = [
        np.kron(np.kron(table, eye), eye),
        np.kron(np.kron(eye, table), eye),
        np.kron(np.kron(eye, eye), table),
    ]
    pair = np.eye(2, dtype=np.float32)
    parts = []
    for d in ([x.T for x in along], along):
        full = np.concatenate([np.kron(pair, -2.0 * x) for x in d], axis=0)
        high = full.astype(jnp.bfloat16)
        parts += [high, (full - high.astype(np.float32)).astype(jnp.bfloat16)]
    return np.concatenate(parts, axis=0)


def halves(x):
    high = x.astype(BF16)
    return high, (x - high.astype(F32)).astype(BF16)


def dot(x, y):
    return jnp.dot(x, y, preferred_element_type=F32)


def dot_full(x, w_high, w_low):
    high, low = halves(x)
    both = dot(jnp.concatenate([high, low], axis=0), w_high)
    return both[: x.shape[0]] + both[x.shape[0] :] + dot(high, w_low)


def lanes_of(x, index):
    return jnp.take_along_axis(x, index, axis=1, mode="promise_in_bounds")


def iota(shape, axis):
    return lax.broadcasted_iota(jnp.int32, shape, axis)


def dot_stacked(x, w_high, w_low):
    high, low = halves(x)
    wide = jnp.concatenate(
        [
            jnp.concatenate([high, high], axis=1),
            jnp.concatenate([low, jnp.zeros_like(low)], axis=1),
        ],
        axis=0,
    )
    both = dot(wide, jnp.concatenate([w_high, w_low], axis=0))
    return both[: x.shape[0]] + both[x.shape[0] :]


def to_rows(x):
    pairs = [jnp.concatenate([x[2 * t], x[2 * t + 1]], axis=1) for t in range(2)]
    pairs.append(jnp.concatenate([x[4], jnp.zeros_like(x[4])], axis=1))
    return jnp.concatenate(pairs, axis=0)


def traces(x, elements):
    lane = iota((elements, LANES), 1)
    block = lane // 32
    m = lane % 16
    parts = []
    for facet in range(6):
        layer = 3 * (facet % 2)
        if facet < 2:
            node = 16 * layer + m
        elif facet < 4:
            node = 16 * (m // 4) + 4 * layer + m % 4
        else:
            node = 4 * m + layer
        at = jnp.where(block == 3, 64, 64 * (lane // 16 % 2) + node)
        a, b, c = (lanes_of(x[elements * t : elements * (t + 1)], at) for t in range(3))
        parts.append(jnp.where(block == 0, a, jnp.where(block == 1, b, c)))
    return jnp.concatenate(parts, axis=0)


def lift(x, elements):
    lane = iota((elements, LANES), 1)
    half, node = lane // 64, lane % 64
    i, j, k = node // 16, node // 4 % 4, node % 4
    rows = []
    for t in range(3):
        base = (2 * t + half) * 16
        total = None
        for axis, (along, m) in enumerate(((i, node % 16), (j, 4 * i + k), (k, 4 * i + j))):
            low, high = (
                lanes_of(x[elements * f : elements * (f + 1)], base + m)
                for f in (2 * axis, 2 * axis + 1)
            )
            term = jnp.where(along == 0, low, jnp.where(along == 3, high, 0.0))
            total = term if total is None else total + term
        rows.append(total)
    return jnp.concatenate(rows, axis=0)


def volume_tables(elements):
    shape = (3 * elements, LANES)
    member = 2 * (iota(shape, 0) // elements) + iota(shape, 1) // 64
    return member


def spread(x, var, elements):
    tile, half = var // 2, var % 2
    part = x[elements * tile : elements * (tile + 1)]
    other = pltpu.roll(part, 64, 1)
    both = jnp.where(iota(part.shape, 1) // 64 == half, part, other)
    return jnp.concatenate([both] * 3, axis=0)


def volume(x, d_high, d_low, elements):
    member = volume_tables(elements)
    ends = jnp.where((member == 0) | (member == 4), 1.0, 0.0)
    pressure = spread(x, 4, elements)
    fluxes = []
    for a in range(3):
        speed = spread(x, 1 + a, elements)
        drift = mean_flow if a == 0 else 0.0
        fluxes.append(
            x * (speed + drift) + ends * speed + jnp.where(member == 1 + a, pressure, 0.0)
        )
    return dot_full(jnp.concatenate(fluxes, axis=1), d_high, d_low)


def volume_back(x, slopes, elements):
    member = volume_tables(elements)
    ends = jnp.where((member == 0) | (member == 4), 1.0, 0.0)
    total = None
    for a in range(3):
        g = slopes[:, LANES * a : LANES * (a + 1)]
        drift = mean_flow if a == 0 else 0.0
        speed = spread(x, 1 + a, elements)
        product = (x + ends) * g
        summed = product[:elements] + product[elements : 2 * elements] + product[2 * elements :]
        summed = summed + pltpu.roll(summed, 64, 1)
        summed = jnp.concatenate([summed] * 3, axis=0)
        term = (speed + drift) * g + jnp.where(member == 1 + a, summed, 0.0)
        term = term + jnp.where(member == 4, spread(g, 1 + a, elements), 0.0)
        total = term if total is None else total + term
    return total


class Faces:
    def __init__(self, elements):
        shape = (6 * elements, LANES)
        lane = iota(shape, 1)
        facet = iota(shape, 0) // elements
        self.node = lane % 16
        self.member = lane // 16
        self.axis = facet // 2
        self.sign = (2 * (facet % 2) - 1).astype(F32)
        self.drift = jnp.where(self.axis == 0, mean_flow, 0.0)
        self.normal = self.member == 1 + self.axis
        self.ends = jnp.where((self.member == 0) | (self.member == 4), 1.0, 0.0)
        self.mirror = jnp.where(self.normal, -1.0, 1.0)
        self.at_speed = (1 + self.axis) * 16 + self.node
        self.at_pressure = 64 + self.node

    def flux(self, q):
        speed = lanes_of(q, self.at_speed)
        pressure = lanes_of(q, self.at_pressure)
        return self.sign * (
            q * (speed + self.drift) + self.ends * speed + jnp.where(self.normal, pressure, 0.0)
        )

    def place(self, axis):
        if axis is None:
            return self.at_speed, self.drift, self.normal
        drift = mean_flow if axis == 0 else 0.0
        return (1 + axis) * 16 + self.node, drift, self.member == 1 + axis

    def ready(self, q, axis=None):
        at, drift, _ = self.place(axis)
        return lanes_of(q, at) + drift, q + self.ends

    def back(self, prepared, w, axis=None):
        at, _, normal = self.place(axis)
        speed, weights = prepared
        product = weights * w
        for shift in (64, 32, 16):
            product = product + pltpu.roll(product, shift, 1)
        term = speed * w + jnp.where(normal, product, 0.0)
        return term + jnp.where(self.member == 4, lanes_of(w, at), 0.0)


def column(values):
    lead, width = values.shape
    x = values.astype(F32)
    x = jnp.concatenate([x, jnp.zeros((8 - lead, width), F32)], axis=0)
    x = x.T
    return jnp.concatenate([x[:, f : f + 1] for f in range(lead)], axis=0).astype(jnp.int32)


def one_hot(flags):
    return jnp.where(flags, 1.0, 0.0).astype(BF16)


def program(net):
    net.greet()
    state = net.load(0)
    elements = state.shape[1]
    n_faces = 6 * elements
    faces = Faces(elements)
    x0 = to_rows(state)
    t0 = traces(x0, elements)
    slots = net.load(1)
    n_slots = slots.shape[1]
    slot_column = column(slots)
    pick = one_hot(slot_column == iota((n_slots, n_faces), 1))
    net.send(0, lambda: dot(pick, t0.astype(BF16)).astype(BF16))

    ext = net.load(2)
    ext_row = jnp.concatenate([ext[f : f + 1] for f in range(6)], axis=1)
    ext_column = column(ext)
    perm_column = column(net.load(3)) + jnp.zeros((n_faces, LANES), jnp.int32)
    wall = ext_column + jnp.zeros((n_faces, LANES), jnp.int32) == n_faces + n_slots
    flip_r = (perm_column & 1) != 0
    flip_s = (perm_column & 2) != 0
    swap = (perm_column & 4) != 0
    base = faces.member * 16
    r, s = faces.node // 4, faces.node % 4
    r_old = jnp.where(swap, s, r)
    s_old = jnp.where(swap, r, s)
    r_old = jnp.where(flip_r, 3 - r_old, r_old)
    s_old = jnp.where(flip_s, 3 - s_old, s_old)
    unorient = base + 4 * r_old + s_old
    to_slots = one_hot(ext_row - n_faces == iota((n_slots, n_faces), 0))

    w = to_rows(net.load(4))
    w_jump = lift_factor * traces(w, elements)
    w_turned = lanes_of(jnp.where(wall, 0.0, w_jump), unorient)

    spare = faces.member >= 5

    def by_axis(x):
        signed = faces.sign * x
        tiles = [jnp.where(faces.axis == a, signed, 0.0) for a in range(3)]
        tiles[0] = jnp.where(spare, pltpu.roll(x, 80, 1), tiles[0])
        tiles[1] = jnp.where(spare, pltpu.roll(x, 32, 1), tiles[1])
        return jnp.concatenate(tiles, axis=1)

    def unpacked(x):
        tiles = [x[:, LANES * a : LANES * (a + 1)] for a in range(3)]
        plain = jnp.where(
            faces.member < 3,
            pltpu.roll(tiles[0], 48, 1),
            jnp.where(spare, 0.0, pltpu.roll(tiles[1], 96, 1)),
        )
        return [jnp.where(spare, 0.0, tiles[0]), jnp.where(spare, 0.0, tiles[1]), tiles[2], plain]

    cot_high, cot_low = halves(by_axis(w_turned))
    net.send(1, lambda: dot(to_slots, cot_high).astype(BF16))

    r_new = jnp.where(flip_r, 3 - r, r)
    s_new = jnp.where(flip_s, 3 - s, s)
    orient = base + jnp.where(swap, 4 * s_new + r_new, 4 * r_new + s_new)
    to_local = one_hot(ext_row == iota((n_faces, n_faces), 0))
    unpick = one_hot(slots == iota((n_faces, n_slots), 0))
    from_local = one_hot(ext_column == iota((n_faces, n_faces), 1))
    from_slots = one_hot(ext_column - n_faces == iota((n_faces, n_slots), 1))

    def outer_local(t):
        both = dot(from_local, jnp.concatenate(halves(t), axis=1))
        return both[:, :LANES] + both[:, LANES:]

    def outer(t, local, received):
        e = lanes_of(local + dot(from_slots, received), orient)
        return jnp.where(wall, t * faces.mirror, e)

    def half(t):
        return 0.5 * faces.flux(t) - t

    local0 = outer_local(t0)
    size = 3 * LANES
    mats = net.load(5)
    d_high, d_low = mats[:size], mats[size : 2 * size]
    b_high, b_low = (
        jnp.concatenate([mats[at + LANES * a : at + LANES * (a + 1)] for a in range(3)], axis=1)
        for at in (2 * size, 3 * size)
    )
    rate0 = volume(x0, d_high, d_low, elements)
    cot_local = dot(to_local, cot_high) + dot(to_local, cot_low) - by_axis(w_jump)
    slopes = dot_stacked(w, b_high, b_low)

    base0 = x0 + step_size * rate0
    half0 = half(t0)
    ready0 = faces.ready(t0)
    e0 = outer(t0, local0, net.wait(0))
    x1 = base0 + step_size * lift_factor * lift(half0 - half(e0), elements)
    t1 = traces(x1, elements)
    net.send(2, lambda: dot(pick, t1.astype(BF16)).astype(BF16))

    back1 = volume_back(x1, slopes, elements)
    wall_out = w_jump - 0.5 * faces.sign * faces.back(faces.ready(t1 * faces.mirror), w_jump)
    t_bar = jnp.where(wall, faces.mirror * wall_out, 0.0)
    ready1 = [faces.ready(t1, a) for a in range(3)]
    ready_e0 = faces.ready(e0)
    cot_all = unpacked(cot_local + dot(unpick, net.wait(1)))
    t_bar = t_bar + cot_all[3]
    for a in range(3):
        t_bar = t_bar - 0.5 * faces.back(ready1[a], cot_all[a], a)
    w1 = 0.5 * w + 0.5 * step_size * (back1 + lift(t_bar, elements))

    w1_jump = lift_factor * traces(w1, elements)
    out_bar = w1_jump - 0.5 * faces.sign * faces.back(ready_e0, w1_jump)
    turned = lanes_of(jnp.where(wall, 0.0, out_bar), unorient)
    turned_high, turned_low = halves(turned)
    net.send(3, lambda: dot(to_slots, turned_high).astype(BF16))

    in_bar = 0.5 * faces.sign * faces.back(ready0, w1_jump) - w1_jump
    in_bar = in_bar + jnp.where(wall, faces.mirror * out_bar, 0.0)
    in_bar = in_bar + dot(to_local, turned_high) + dot(to_local, turned_low)
    slopes1 = dot_stacked(w1, b_high, b_low)
    back0 = volume_back(x0, slopes1, elements)
    start = w1 - 0.5 * w + step_size * back0

    local1 = outer_local(t1)
    rate1 = volume(x1, d_high, d_low, elements)
    half1 = half(t1)
    e1 = outer(t1, local1, net.wait(2))
    rate1 = rate1 + lift_factor * lift(half1 - half(e1), elements)
    net.output(0, 0.5 * (x1 - x0) + 0.5 * step_size * rate1)

    in_bar = in_bar + dot(unpick, net.wait(3))
    start = start + step_size * lift(in_bar, elements)
    net.output(1, start)


class Net:
    def __init__(
        self, n_dom, n_sub, inputs, held, send_bufs, recv_bufs, send_sem, recv_sem, load_sem
    ):
        self.n_dom, self.n_sub = n_dom, n_sub
        self.dom, self.sub = lax.axis_index("dom"), lax.axis_index("sub")
        self.send_bufs, self.recv_bufs = send_bufs, recv_bufs
        self.send_sem, self.recv_sem = send_sem, recv_sem
        self.greeted = False
        self.held = held
        self.loads = [
            pltpu.make_async_copy(inputs[n], held[n], load_sem.at[n]) for n in range(len(held))
        ]
        for load in self.loads:
            load.start()

    def load(self, which):
        self.loads[which].wait()
        return self.held[which][...]

    def partners(self, way=1):
        first = way * (2 * lax.rem(self.dom, 2) - 1)
        for group, ahead in ((1 + first, True), (1 - first, True), (1, False)):
            for j in range(self.n_sub):
                if ahead or j != 0:
                    yield group, lax.rem(self.sub + j, self.n_sub)

    def neighbour(self, steps):
        return lax.rem(self.dom + steps + self.n_dom, self.n_dom)

    def greet(self):
        barrier = pltpu.get_barrier_semaphore()
        for group, other in self.partners():
            pl.semaphore_signal(
                barrier,
                inc=1,
                device_id=(self.neighbour(group - 1), other),
                device_id_type=pl.DeviceIdType.MESH,
            )

    def copies(self, phase):
        source, target = self.send_bufs[phase], self.recv_bufs[phase]
        size = source.shape[0] // (3 * self.n_sub)
        way = 1 if phase % 2 == 0 else -1
        for group, other in self.partners(way):
            there = pl.multiple_of((group * self.n_sub + other) * size, size)
            here = pl.multiple_of((group * self.n_sub + self.sub) * size, size)
            yield pltpu.make_async_remote_copy(
                src_ref=source.at[pl.ds(there, size)],
                dst_ref=target.at[pl.ds(here, size)],
                send_sem=self.send_sem.at[phase, group * self.n_sub + other],
                recv_sem=self.recv_sem.at[phase, group * self.n_sub + self.sub],
                device_id=(self.neighbour(way * (group - 1)), other),
                device_id_type=pl.DeviceIdType.MESH,
            )

    def send(self, phase, make):
        source, target = self.send_bufs[phase], self.recv_bufs[phase]
        source[...] = make()
        if not self.greeted:
            pl.semaphore_wait(pltpu.get_barrier_semaphore(), 3 * self.n_sub - 1)
            self.greeted = True
        for copy in self.copies(phase):
            copy.start()
        size = source.shape[0] // (3 * self.n_sub)
        own = pl.ds(pl.multiple_of((self.n_sub + self.sub) * size, size), size)
        target[own] = source[own]

    def wait(self, phase):
        source, target = self.send_bufs[phase], self.recv_bufs[phase]
        size = source.shape[0] // (3 * self.n_sub)
        for group, other in self.partners():
            rows = pl.ds(pl.multiple_of((group * self.n_sub + other) * size, size), size)
            index = group * self.n_sub + other
            pltpu.make_async_remote_copy(
                src_ref=source.at[rows],
                dst_ref=target.at[rows],
                send_sem=self.send_sem.at[phase, index],
                recv_sem=self.recv_sem.at[phase, index],
                device_id=(self.neighbour(group - 1), other),
                device_id_type=pl.DeviceIdType.MESH,
            ).wait_recv()
        return target[...]

    def finish(self):
        for phase in range(4):
            for copy in self.copies(phase):
                copy.wait_send()
        for store in self.stores:
            store.wait()

    def output(self, which, x):
        elements = x.shape[0] // 3
        for member in range(5):
            tile, half = member // 2, member % 2
            self.staged[5 * which + member] = x[
                elements * tile : elements * (tile + 1), 64 * half : 64 * (half + 1)
            ]
        self.stores[which].start()


def kernel(n_dom, n_sub, *refs):
    inputs, out, held, staged = refs[:6], refs[6], refs[7:13], refs[13]
    send_bufs, recv_bufs = refs[14:18], refs[18:22]
    send_sem, recv_sem, load_sem, store_sem = refs[22:]
    net = Net(n_dom, n_sub, inputs, held, send_bufs, recv_bufs, send_sem, recv_sem, load_sem)
    net.staged = staged
    net.stores = [
        pltpu.make_async_copy(
            staged.at[pl.ds(5 * n, 5)], out.at[pl.ds(5 * n, 5)], store_sem.at[n]
        )
        for n in range(2)
    ]
    program(net)
    net.finish()


def solution(mesh):
    n_dom, n_sub = mesh.shape["dom"], mesh.shape["sub"]
    mats = constants()

    def shards(state, final, send_slot, ext_index, ext_perm):
        n_slots = send_slot.shape[1]
        widths = (LANES, 3 * LANES, LANES, LANES)
        buffers = [pltpu.VMEM((n_slots, width), BF16) for width in widths]
        operands = [
            state.transpose(0, 2, 1),
            send_slot,
            ext_index,
            ext_perm,
            final.transpose(0, 2, 1),
            jnp.asarray(mats),
        ]
        elements = state.shape[2]
        result = jax.ShapeDtypeStruct((10, elements, 64), F32)
        hbm = pl.BlockSpec(memory_space=pltpu.HBM)
        change = pl.pallas_call(
            lambda *refs: kernel(n_dom, n_sub, *refs),
            out_shape=result,
            in_specs=[hbm] * 6,
            out_specs=hbm,
            scratch_shapes=[pltpu.VMEM(x.shape, x.dtype) for x in operands]
            + [pltpu.VMEM((10, elements, 64), F32)]
            + buffers
            + buffers
            + [
                pltpu.SemaphoreType.DMA((4, 3 * n_sub)),
                pltpu.SemaphoreType.DMA((4, 3 * n_sub)),
                pltpu.SemaphoreType.DMA((6,)),
                pltpu.SemaphoreType.DMA((2,)),
            ],
            compiler_params=pltpu.CompilerParams(
                collective_id=0, has_side_effects=True, vmem_limit_bytes=60 * 1024 * 1024
            ),
        )(*operands)
        change = change.transpose(0, 2, 1)
        return state + change[:5], final + change[5:]

    return jax.shard_map(
        shards,
        mesh=mesh,
        in_specs=(
            P(None, None, ("dom", "sub")),
            P(None, None, ("dom", "sub")),
            P(("dom", "sub"), None),
            P(None, ("dom", "sub")),
            P(None, ("dom", "sub")),
        ),
        out_specs=(P(None, None, ("dom", "sub")), P(None, None, ("dom", "sub"))),
        check_vma=False,
    )
```

```python
import jax
import jax.numpy as jnp
import numpy as np
from jax import lax
from jax.experimental import pallas as pl
from jax.experimental.pallas import tpu as pltpu
from jax.sharding import PartitionSpec as P

step_size = 0.02
mean_flow = 0.3
lift_factor = 12.0
LANES = 128
F32 = jnp.float32
BF16 = jnp.bfloat16


def derivative_table():
    points = np.array([-1.0, -1.0 / np.sqrt(5.0), 1.0 / np.sqrt(5.0), 1.0])
    products = np.array(
        [
            np.prod([points[target] - points[source] for source in range(4) if source != target])
            for target in range(4)
        ]
    )
    result = np.zeros((4, 4))
    for target in range(4):
        for source in range(4):
            if target != source:
                result[target, source] = products[target] / (
                    products[source] * (points[target] - points[source])
                )
        result[target, target] = -np.sum(result[target])
    return result.astype(np.float32)


def constants():
    table = derivative_table()
    eye = np.eye(4, dtype=np.float32)
    along = [
        np.kron(np.kron(table, eye), eye),
        np.kron(np.kron(eye, table), eye),
        np.kron(np.kron(eye, eye), table),
    ]
    pair = np.eye(2, dtype=np.float32)
    parts = []
    for d in ([x.T for x in along], along):
        full = np.concatenate([np.kron(pair, -2.0 * x) for x in d], axis=0)
        high = full.astype(jnp.bfloat16)
        parts += [high, (full - high.astype(np.float32)).astype(jnp.bfloat16)]
    return np.concatenate(parts, axis=0)


def halves(x):
    high = x.astype(BF16)
    return high, (x - high.astype(F32)).astype(BF16)


def dot(x, y):
    return jnp.dot(x, y, preferred_element_type=F32)


def dot_full(x, w_high, w_low):
    high, low = halves(x)
    both = dot(jnp.concatenate([high, low], axis=0), w_high)
    return both[: x.shape[0]] + both[x.shape[0] :] + dot(high, w_low)


def lanes_of(x, index):
    return jnp.take_along_axis(x, index, axis=1, mode="promise_in_bounds")


def iota(shape, axis):
    return lax.broadcasted_iota(jnp.int32, shape, axis)


def dot_stacked(x, w_high, w_low):
    high, low = halves(x)
    wide = jnp.concatenate(
        [
            jnp.concatenate([high, high], axis=1),
            jnp.concatenate([low, jnp.zeros_like(low)], axis=1),
        ],
        axis=0,
    )
    both = dot(wide, jnp.concatenate([w_high, w_low], axis=0))
    return both[: x.shape[0]] + both[x.shape[0] :]


def to_rows(x):
    pairs = [jnp.concatenate([x[2 * t], x[2 * t + 1]], axis=1) for t in range(2)]
    pairs.append(jnp.concatenate([x[4], jnp.zeros_like(x[4])], axis=1))
    return jnp.concatenate(pairs, axis=0)


def traces(x, elements):
    lane = iota((elements, LANES), 1)
    block = lane // 32
    m = lane % 16
    parts = []
    for facet in range(6):
        layer = 3 * (facet % 2)
        if facet < 2:
            node = 16 * layer + m
        elif facet < 4:
            node = 16 * (m // 4) + 4 * layer + m % 4
        else:
            node = 4 * m + layer
        at = jnp.where(block == 3, 64, 64 * (lane // 16 % 2) + node)
        a, b, c = (lanes_of(x[elements * t : elements * (t + 1)], at) for t in range(3))
        parts.append(jnp.where(block == 0, a, jnp.where(block == 1, b, c)))
    return jnp.concatenate(parts, axis=0)


def lift(x, elements):
    lane = iota((elements, LANES), 1)
    half, node = lane // 64, lane % 64
    i, j, k = node // 16, node // 4 % 4, node % 4
    rows = []
    for t in range(3):
        base = (2 * t + half) * 16
        total = None
        for axis, (along, m) in enumerate(((i, node % 16), (j, 4 * i + k), (k, 4 * i + j))):
            low, high = (
                lanes_of(x[elements * f : elements * (f + 1)], base + m)
                for f in (2 * axis, 2 * axis + 1)
            )
            term = jnp.where(along == 0, low, jnp.where(along == 3, high, 0.0))
            total = term if total is None else total + term
        rows.append(total)
    return jnp.concatenate(rows, axis=0)


def volume_tables(elements):
    shape = (3 * elements, LANES)
    member = 2 * (iota(shape, 0) // elements) + iota(shape, 1) // 64
    return member


def spread(x, var, elements):
    tile, half = var // 2, var % 2
    part = x[elements * tile : elements * (tile + 1)]
    other = pltpu.roll(part, 64, 1)
    both = jnp.where(iota(part.shape, 1) // 64 == half, part, other)
    return jnp.concatenate([both] * 3, axis=0)


def volume(x, d_high, d_low, elements):
    member = volume_tables(elements)
    ends = jnp.where((member == 0) | (member == 4), 1.0, 0.0)
    pressure = spread(x, 4, elements)
    fluxes = []
    for a in range(3):
        speed = spread(x, 1 + a, elements)
        drift = mean_flow if a == 0 else 0.0
        fluxes.append(
            x * (speed + drift) + ends * speed + jnp.where(member == 1 + a, pressure, 0.0)
        )
    return dot_full(jnp.concatenate(fluxes, axis=1), d_high, d_low)


def volume_back(x, slopes, elements):
    member = volume_tables(elements)
    ends = jnp.where((member == 0) | (member == 4), 1.0, 0.0)
    total = None
    for a in range(3):
        g = slopes[:, LANES * a : LANES * (a + 1)]
        drift = mean_flow if a == 0 else 0.0
        speed = spread(x, 1 + a, elements)
        product = (x + ends) * g
        summed = product[:elements] + product[elements : 2 * elements] + product[2 * elements :]
        summed = summed + pltpu.roll(summed, 64, 1)
        summed = jnp.concatenate([summed] * 3, axis=0)
        term = (speed + drift) * g + jnp.where(member == 1 + a, summed, 0.0)
        term = term + jnp.where(member == 4, spread(g, 1 + a, elements), 0.0)
        total = term if total is None else total + term
    return total


class Faces:
    def __init__(self, elements):
        shape = (6 * elements, LANES)
        lane = iota(shape, 1)
        facet = iota(shape, 0) // elements
        self.node = lane % 16
        self.member = lane // 16
        self.axis = facet // 2
        self.sign = (2 * (facet % 2) - 1).astype(F32)
        self.drift = jnp.where(self.axis == 0, mean_flow, 0.0)
        self.normal = self.member == 1 + self.axis
        self.ends = jnp.where((self.member == 0) | (self.member == 4), 1.0, 0.0)
        self.mirror = jnp.where(self.normal, -1.0, 1.0)
        self.at_speed = (1 + self.axis) * 16 + self.node
        self.at_pressure = 64 + self.node

    def flux(self, q):
        speed = lanes_of(q, self.at_speed)
        pressure = lanes_of(q, self.at_pressure)
        return self.sign * (
            q * (speed + self.drift) + self.ends * speed + jnp.where(self.normal, pressure, 0.0)
        )

    def place(self, axis):
        if axis is None:
            return self.at_speed, self.drift, self.normal
        drift = mean_flow if axis == 0 else 0.0
        return (1 + axis) * 16 + self.node, drift, self.member == 1 + axis

    def ready(self, q, axis=None):
        at, drift, _ = self.place(axis)
        return lanes_of(q, at) + drift, q + self.ends

    def back(self, prepared, w, axis=None):
        at, _, normal = self.place(axis)
        speed, weights = prepared
        product = weights * w
        for shift in (64, 32, 16):
            product = product + pltpu.roll(product, shift, 1)
        term = speed * w + jnp.where(normal, product, 0.0)
        return term + jnp.where(self.member == 4, lanes_of(w, at), 0.0)


def column(values):
    lead, width = values.shape
    x = values.astype(F32)
    x = jnp.concatenate([x, jnp.zeros((8 - lead, width), F32)], axis=0)
    x = x.T
    return jnp.concatenate([x[:, f : f + 1] for f in range(lead)], axis=0).astype(jnp.int32)


def one_hot(flags):
    return jnp.where(flags, 1.0, 0.0).astype(BF16)


def program(net):
    net.greet()
    state = net.load(0)
    elements = state.shape[1]
    n_faces = 6 * elements
    faces = Faces(elements)
    x0 = to_rows(state)
    t0 = traces(x0, elements)
    slots = net.load(1)
    n_slots = slots.shape[1]
    slot_column = column(slots)
    pick = one_hot(slot_column == iota((n_slots, n_faces), 1))
    net.send(0, lambda: dot(pick, t0.astype(BF16)).astype(BF16))

    ext = net.load(2)
    ext_row = jnp.concatenate([ext[f : f + 1] for f in range(6)], axis=1)
    ext_column = column(ext)
    perm_column = column(net.load(3)) + jnp.zeros((n_faces, LANES), jnp.int32)
    wall = ext_column + jnp.zeros((n_faces, LANES), jnp.int32) == n_faces + n_slots
    flip_r = (perm_column & 1) != 0
    flip_s = (perm_column & 2) != 0
    swap = (perm_column & 4) != 0
    base = faces.member * 16
    r, s = faces.node // 4, faces.node % 4
    r_old = jnp.where(swap, s, r)
    s_old = jnp.where(swap, r, s)
    r_old = jnp.where(flip_r, 3 - r_old, r_old)
    s_old = jnp.where(flip_s, 3 - s_old, s_old)
    unorient = base + 4 * r_old + s_old
    to_slots = one_hot(ext_row - n_faces == iota((n_slots, n_faces), 0))

    w = to_rows(net.load(4))
    w_jump = lift_factor * traces(w, elements)
    w_turned = lanes_of(jnp.where(wall, 0.0, w_jump), unorient)

    spare = faces.member >= 5

    def by_axis(x):
        signed = faces.sign * x
        tiles = [jnp.where(faces.axis == a, signed, 0.0) for a in range(3)]
        tiles[0] = jnp.where(spare, pltpu.roll(x, 80, 1), tiles[0])
        tiles[1] = jnp.where(spare, pltpu.roll(x, 32, 1), tiles[1])
        return jnp.concatenate(tiles, axis=1)

    def unpacked(x):
        tiles = [x[:, LANES * a : LANES * (a + 1)] for a in range(3)]
        plain = jnp.where(
            faces.member < 3,
            pltpu.roll(tiles[0], 48, 1),
            jnp.where(spare, 0.0, pltpu.roll(tiles[1], 96, 1)),
        )
        return [jnp.where(spare, 0.0, tiles[0]), jnp.where(spare, 0.0, tiles[1]), tiles[2], plain]

    cot_high, cot_low = halves(by_axis(w_turned))
    net.send(1, lambda: dot(to_slots, cot_high).astype(BF16))

    r_new = jnp.where(flip_r, 3 - r, r)
    s_new = jnp.where(flip_s, 3 - s, s)
    orient = base + jnp.where(swap, 4 * s_new + r_new, 4 * r_new + s_new)
    to_local = one_hot(ext_row == iota((n_faces, n_faces), 0))
    unpick = one_hot(slots == iota((n_faces, n_slots), 0))
    from_local = one_hot(ext_column == iota((n_faces, n_faces), 1))
    from_slots = one_hot(ext_column - n_faces == iota((n_faces, n_slots), 1))

    def outer_local(t):
        both = dot(from_local, jnp.concatenate(halves(t), axis=1))
        return both[:, :LANES] + both[:, LANES:]

    def outer(t, local, received):
        e = lanes_of(local + dot(from_slots, received), orient)
        return jnp.where(wall, t * faces.mirror, e)

    def half(t):
        return 0.5 * faces.flux(t) - t

    local0 = outer_local(t0)
    size = 3 * LANES
    mats = net.load(5)
    d_high, d_low = mats[:size], mats[size : 2 * size]
    b_high, b_low = (
        jnp.concatenate([mats[at + LANES * a : at + LANES * (a + 1)] for a in range(3)], axis=1)
        for at in (2 * size, 3 * size)
    )
    rate0 = volume(x0, d_high, d_low, elements)
    cot_local = dot(to_local, cot_high) + dot(to_local, cot_low) - by_axis(w_jump)
    slopes = dot_stacked(w, b_high, b_low)

    base0 = x0 + step_size * rate0
    half0 = half(t0)
    ready0 = faces.ready(t0)
    e0 = outer(t0, local0, net.wait(0))
    x1 = base0 + step_size * lift_factor * lift(half0 - half(e0), elements)
    t1 = traces(x1, elements)
    net.send(2, lambda: dot(pick, t1.astype(BF16)).astype(BF16))

    back1 = volume_back(x1, slopes, elements)
    wall_out = w_jump - 0.5 * faces.sign * faces.back(faces.ready(t1 * faces.mirror), w_jump)
    t_bar = jnp.where(wall, faces.mirror * wall_out, 0.0)
    ready1 = [faces.ready(t1, a) for a in range(3)]
    ready_e0 = faces.ready(e0)
    cot_all = unpacked(cot_local + dot(unpick, net.wait(1)))
    t_bar = t_bar + cot_all[3]
    for a in range(3):
        t_bar = t_bar - 0.5 * faces.back(ready1[a], cot_all[a], a)
    w1 = 0.5 * w + 0.5 * step_size * (back1 + lift(t_bar, elements))

    w1_jump = lift_factor * traces(w1, elements)
    out_bar = w1_jump - 0.5 * faces.sign * faces.back(ready_e0, w1_jump)
    turned = lanes_of(jnp.where(wall, 0.0, out_bar), unorient)
    turned_high, turned_low = halves(turned)
    net.send(3, lambda: dot(to_slots, turned_high).astype(BF16))

    in_bar = 0.5 * faces.sign * faces.back(ready0, w1_jump) - w1_jump
    in_bar = in_bar + jnp.where(wall, faces.mirror * out_bar, 0.0)
    in_bar = in_bar + dot(to_local, turned_high) + dot(to_local, turned_low)
    slopes1 = dot_stacked(w1, b_high, b_low)
    back0 = volume_back(x0, slopes1, elements)
    start = 0.5 * w + w1 + step_size * back0

    local1 = outer_local(t1)
    rate1 = volume(x1, d_high, d_low, elements)
    half1 = half(t1)
    e1 = outer(t1, local1, net.wait(2))
    rate1 = rate1 + lift_factor * lift(half1 - half(e1), elements)
    net.output(0, 0.5 * x0 + 0.5 * (x1 + step_size * rate1))
    net.sent((0, 1, 2))

    in_bar = in_bar + dot(unpick, net.wait(3))
    start = start + step_size * lift(in_bar, elements)
    net.output(1, start)


class Net:
    def __init__(
        self, n_dom, n_sub, inputs, held, send_bufs, recv_bufs, send_sem, recv_sem, load_sem
    ):
        self.n_dom, self.n_sub = n_dom, n_sub
        self.dom, self.sub = lax.axis_index("dom"), lax.axis_index("sub")
        self.send_bufs, self.recv_bufs = send_bufs, recv_bufs
        self.send_sem, self.recv_sem = send_sem, recv_sem
        self.greeted = False
        self.held = held
        self.loads = [
            pltpu.make_async_copy(inputs[n], held[n], load_sem.at[n]) for n in range(len(held))
        ]
        for load in self.loads:
            load.start()

    def load(self, which):
        self.loads[which].wait()
        return self.held[which][...]

    def partners(self, way=1):
        first = way * (2 * lax.rem(self.dom, 2) - 1)
        for group, ahead in ((1 + first, True), (1 - first, True), (1, False)):
            for j in range(self.n_sub):
                if ahead or j != 0:
                    yield group, lax.rem(self.sub + j, self.n_sub)

    def neighbour(self, steps):
        return lax.rem(self.dom + steps + self.n_dom, self.n_dom)

    def greet(self):
        barrier = pltpu.get_barrier_semaphore()
        for group, other in self.partners():
            pl.semaphore_signal(
                barrier,
                inc=1,
                device_id=(self.neighbour(group - 1), other),
                device_id_type=pl.DeviceIdType.MESH,
            )

    def copies(self, phase):
        source, target = self.send_bufs[phase], self.recv_bufs[phase]
        size = source.shape[0] // (3 * self.n_sub)
        way = 1 if phase % 2 == 0 else -1
        for group, other in self.partners(way):
            there = pl.multiple_of((group * self.n_sub + other) * size, size)
            here = pl.multiple_of((group * self.n_sub + self.sub) * size, size)
            yield pltpu.make_async_remote_copy(
                src_ref=source.at[pl.ds(there, size)],
                dst_ref=target.at[pl.ds(here, size)],
                send_sem=self.send_sem.at[phase, group * self.n_sub + other],
                recv_sem=self.recv_sem.at[phase, group * self.n_sub + self.sub],
                device_id=(self.neighbour(way * (group - 1)), other),
                device_id_type=pl.DeviceIdType.MESH,
            )

    def send(self, phase, make):
        source, target = self.send_bufs[phase], self.recv_bufs[phase]
        source[...] = make()
        if not self.greeted:
            pl.semaphore_wait(pltpu.get_barrier_semaphore(), 3 * self.n_sub - 1)
            self.greeted = True
        for copy in self.copies(phase):
            copy.start()
        size = source.shape[0] // (3 * self.n_sub)
        own = pl.ds(pl.multiple_of((self.n_sub + self.sub) * size, size), size)
        target[own] = source[own]

    def wait(self, phase):
        source, target = self.send_bufs[phase], self.recv_bufs[phase]
        size = source.shape[0] // (3 * self.n_sub)
        for group, other in self.partners():
            rows = pl.ds(pl.multiple_of((group * self.n_sub + other) * size, size), size)
            index = group * self.n_sub + other
            pltpu.make_async_remote_copy(
                src_ref=source.at[rows],
                dst_ref=target.at[rows],
                send_sem=self.send_sem.at[phase, index],
                recv_sem=self.recv_sem.at[phase, index],
                device_id=(self.neighbour(group - 1), other),
                device_id_type=pl.DeviceIdType.MESH,
            ).wait_recv()
        return target[...]

    def sent(self, phases):
        for phase in phases:
            for copy in self.copies(phase):
                copy.wait_send()

    def finish(self):
        self.sent((3,))
        for store in self.stores:
            store.wait()

    def output(self, which, x):
        elements = x.shape[0] // 3
        for member in range(5):
            tile, half = member // 2, member % 2
            self.staged[5 * which + member] = x[
                elements * tile : elements * (tile + 1), 64 * half : 64 * (half + 1)
            ]
        self.stores[which].start()


def kernel(n_dom, n_sub, *refs):
    inputs, out, held, staged = refs[:6], refs[6], refs[7:13], refs[13]
    send_bufs, recv_bufs = refs[14:18], refs[18:22]
    send_sem, recv_sem, load_sem, store_sem = refs[22:]
    net = Net(n_dom, n_sub, inputs, held, send_bufs, recv_bufs, send_sem, recv_sem, load_sem)
    net.staged = staged
    net.stores = [
        pltpu.make_async_copy(
            staged.at[pl.ds(5 * n, 5)], out.at[pl.ds(5 * n, 5)], store_sem.at[n]
        )
        for n in range(2)
    ]
    program(net)
    net.finish()


def hand_out(both, first, second, sems):
    copies = [
        pltpu.make_async_copy(both.at[pl.ds(5 * n, 5)], out, sems.at[n])
        for n, out in enumerate((first, second))
    ]
    for copy in copies:
        copy.start()
    for copy in copies:
        copy.wait()


def solution(mesh):
    n_dom, n_sub = mesh.shape["dom"], mesh.shape["sub"]
    mats = constants()

    def shards(state, final, send_slot, ext_index, ext_perm):
        n_slots = send_slot.shape[1]
        widths = (LANES, 3 * LANES, LANES, LANES)
        buffers = [pltpu.VMEM((n_slots, width), BF16) for width in widths]
        operands = [
            state.transpose(0, 2, 1),
            send_slot,
            ext_index,
            ext_perm,
            final.transpose(0, 2, 1),
            jnp.asarray(mats),
        ]
        elements = state.shape[2]
        result = jax.ShapeDtypeStruct((10, elements, 64), F32)
        hbm = pl.BlockSpec(memory_space=pltpu.HBM)
        both = pl.pallas_call(
            lambda *refs: kernel(n_dom, n_sub, *refs),
            out_shape=result,
            in_specs=[hbm] * 6,
            out_specs=hbm,
            scratch_shapes=[pltpu.VMEM(x.shape, x.dtype) for x in operands]
            + [pltpu.VMEM((10, elements, 64), F32)]
            + buffers
            + buffers
            + [
                pltpu.SemaphoreType.DMA((4, 3 * n_sub)),
                pltpu.SemaphoreType.DMA((4, 3 * n_sub)),
                pltpu.SemaphoreType.DMA((6,)),
                pltpu.SemaphoreType.DMA((2,)),
            ],
            compiler_params=pltpu.CompilerParams(
                collective_id=0, has_side_effects=True, vmem_limit_bytes=60 * 1024 * 1024
            ),
        )(*operands)
        single = jax.ShapeDtypeStruct((5, elements, 64), F32)
        outs = pl.pallas_call(
            hand_out,
            out_shape=(single, single),
            in_specs=[hbm],
            out_specs=(hbm, hbm),
            scratch_shapes=[pltpu.SemaphoreType.DMA((2,))],
            compiler_params=pltpu.CompilerParams(vmem_limit_bytes=60 * 1024 * 1024),
        )(both)
        return tuple(x.transpose(0, 2, 1) for x in outs)

    return jax.shard_map(
        shards,
        mesh=mesh,
        in_specs=(
            P(None, None, ("dom", "sub")),
            P(None, None, ("dom", "sub")),
            P(("dom", "sub"), None),
            P(None, ("dom", "sub")),
            P(None, ("dom", "sub")),
        ),
        out_specs=(P(None, None, ("dom", "sub")), P(None, None, ("dom", "sub"))),
        check_vma=False,
    )
```

```python
import jax
import jax.numpy as jnp
import numpy as np
from jax import lax
from jax.experimental import pallas as pl
from jax.experimental.pallas import tpu as pltpu
from jax.sharding import PartitionSpec as P

step_size = 0.02
mean_flow = 0.3
lift_factor = 12.0
LANES = 128
F32 = jnp.float32
BF16 = jnp.bfloat16


def derivative_table():
    points = np.array([-1.0, -1.0 / np.sqrt(5.0), 1.0 / np.sqrt(5.0), 1.0])
    products = np.array(
        [
            np.prod([points[target] - points[source] for source in range(4) if source != target])
            for target in range(4)
        ]
    )
    result = np.zeros((4, 4))
    for target in range(4):
        for source in range(4):
            if target != source:
                result[target, source] = products[target] / (
                    products[source] * (points[target] - points[source])
                )
        result[target, target] = -np.sum(result[target])
    return result.astype(np.float32)


def constants():
    table = derivative_table()
    eye = np.eye(4, dtype=np.float32)
    along = [
        np.kron(np.kron(table, eye), eye),
        np.kron(np.kron(eye, table), eye),
        np.kron(np.kron(eye, eye), table),
    ]
    pair = np.eye(2, dtype=np.float32)
    parts = []
    for d in ([x.T for x in along], along):
        full = np.concatenate([np.kron(pair, -2.0 * x) for x in d], axis=0)
        high = full.astype(jnp.bfloat16)
        parts += [high, (full - high.astype(np.float32)).astype(jnp.bfloat16)]
    return np.concatenate(parts, axis=0)


def halves(x):
    high = x.astype(BF16)
    return high, (x - high.astype(F32)).astype(BF16)


def dot(x, y):
    return jnp.dot(x, y, preferred_element_type=F32)


def dot_full(x, w_high, w_low):
    high, low = halves(x)
    both = dot(jnp.concatenate([high, low], axis=0), w_high)
    return both[: x.shape[0]] + both[x.shape[0] :] + dot(high, w_low)


def lanes_of(x, index):
    return jnp.take_along_axis(x, index, axis=1, mode="promise_in_bounds")


def iota(shape, axis):
    return lax.broadcasted_iota(jnp.int32, shape, axis)


def dot_stacked(x, w_high, w_low):
    high, low = halves(x)
    wide = jnp.concatenate(
        [
            jnp.concatenate([high, high], axis=1),
            jnp.concatenate([low, jnp.zeros_like(low)], axis=1),
        ],
        axis=0,
    )
    both = dot(wide, jnp.concatenate([w_high, w_low], axis=0))
    return both[: x.shape[0]] + both[x.shape[0] :]


def to_rows(x):
    pairs = [jnp.concatenate([x[2 * t], x[2 * t + 1]], axis=1) for t in range(2)]
    pairs.append(jnp.concatenate([x[4], jnp.zeros_like(x[4])], axis=1))
    return jnp.concatenate(pairs, axis=0)


def traces(x, elements):
    lane = iota((elements, LANES), 1)
    block = lane // 32
    m = lane % 16
    parts = []
    for facet in range(6):
        layer = 3 * (facet % 2)
        if facet < 2:
            node = 16 * layer + m
        elif facet < 4:
            node = 16 * (m // 4) + 4 * layer + m % 4
        else:
            node = 4 * m + layer
        at = jnp.where(block == 3, 64, 64 * (lane // 16 % 2) + node)
        a, b, c = (lanes_of(x[elements * t : elements * (t + 1)], at) for t in range(3))
        parts.append(jnp.where(block == 0, a, jnp.where(block == 1, b, c)))
    return jnp.concatenate(parts, axis=0)


def lift(x, elements):
    lane = iota((elements, LANES), 1)
    half, node = lane // 64, lane % 64
    i, j, k = node // 16, node // 4 % 4, node % 4
    rows = []
    for t in range(3):
        base = (2 * t + half) * 16
        total = None
        for axis, (along, m) in enumerate(((i, node % 16), (j, 4 * i + k), (k, 4 * i + j))):
            low, high = (
                lanes_of(x[elements * f : elements * (f + 1)], base + m)
                for f in (2 * axis, 2 * axis + 1)
            )
            term = jnp.where(along == 0, low, jnp.where(along == 3, high, 0.0))
            total = term if total is None else total + term
        rows.append(total)
    return jnp.concatenate(rows, axis=0)


def volume_tables(elements):
    shape = (3 * elements, LANES)
    member = 2 * (iota(shape, 0) // elements) + iota(shape, 1) // 64
    return member


def spread(x, var, elements):
    tile, half = var // 2, var % 2
    part = x[elements * tile : elements * (tile + 1)]
    other = pltpu.roll(part, 64, 1)
    both = jnp.where(iota(part.shape, 1) // 64 == half, part, other)
    return jnp.concatenate([both] * 3, axis=0)


def volume(x, d_high, d_low, elements):
    member = volume_tables(elements)
    ends = jnp.where((member == 0) | (member == 4), 1.0, 0.0)
    pressure = spread(x, 4, elements)
    fluxes = []
    for a in range(3):
        speed = spread(x, 1 + a, elements)
        drift = mean_flow if a == 0 else 0.0
        fluxes.append(
            x * (speed + drift) + ends * speed + jnp.where(member == 1 + a, pressure, 0.0)
        )
    return dot_full(jnp.concatenate(fluxes, axis=1), d_high, d_low)


def volume_back(x, slopes, elements):
    member = volume_tables(elements)
    ends = jnp.where((member == 0) | (member == 4), 1.0, 0.0)
    total = None
    for a in range(3):
        g = slopes[:, LANES * a : LANES * (a + 1)]
        drift = mean_flow if a == 0 else 0.0
        speed = spread(x, 1 + a, elements)
        product = (x + ends) * g
        summed = product[:elements] + product[elements : 2 * elements] + product[2 * elements :]
        summed = summed + pltpu.roll(summed, 64, 1)
        summed = jnp.concatenate([summed] * 3, axis=0)
        term = (speed + drift) * g + jnp.where(member == 1 + a, summed, 0.0)
        term = term + jnp.where(member == 4, spread(g, 1 + a, elements), 0.0)
        total = term if total is None else total + term
    return total


class Faces:
    def __init__(self, elements):
        shape = (6 * elements, LANES)
        lane = iota(shape, 1)
        facet = iota(shape, 0) // elements
        self.node = lane % 16
        self.member = lane // 16
        self.axis = facet // 2
        self.sign = (2 * (facet % 2) - 1).astype(F32)
        self.drift = jnp.where(self.axis == 0, mean_flow, 0.0)
        self.normal = self.member == 1 + self.axis
        self.ends = jnp.where((self.member == 0) | (self.member == 4), 1.0, 0.0)
        self.mirror = jnp.where(self.normal, -1.0, 1.0)
        self.at_speed = (1 + self.axis) * 16 + self.node
        self.at_pressure = 64 + self.node

    def flux(self, q):
        speed = lanes_of(q, self.at_speed)
        pressure = lanes_of(q, self.at_pressure)
        return self.sign * (
            q * (speed + self.drift) + self.ends * speed + jnp.where(self.normal, pressure, 0.0)
        )

    def place(self, axis):
        if axis is None:
            return self.at_speed, self.drift, self.normal
        drift = mean_flow if axis == 0 else 0.0
        return (1 + axis) * 16 + self.node, drift, self.member == 1 + axis

    def ready(self, q, axis=None):
        at, drift, _ = self.place(axis)
        return lanes_of(q, at) + drift, q + self.ends

    def back(self, prepared, w, axis=None):
        at, _, normal = self.place(axis)
        speed, weights = prepared
        product = weights * w
        for shift in (64, 32, 16):
            product = product + pltpu.roll(product, shift, 1)
        term = speed * w + jnp.where(normal, product, 0.0)
        return term + jnp.where(self.member == 4, lanes_of(w, at), 0.0)


def column(values):
    lead, width = values.shape
    x = values.astype(F32)
    x = jnp.concatenate([x, jnp.zeros((8 - lead, width), F32)], axis=0)
    x = x.T
    return jnp.concatenate([x[:, f : f + 1] for f in range(lead)], axis=0).astype(jnp.int32)


def one_hot(flags):
    return jnp.where(flags, 1.0, 0.0).astype(BF16)


def program(net):
    net.greet()
    state = net.load(0)
    elements = state.shape[1]
    n_faces = 6 * elements
    faces = Faces(elements)
    x0 = to_rows(state)
    t0 = traces(x0, elements)
    slots = net.load(1)
    n_slots = slots.shape[1]
    slot_column = column(slots)
    pick = one_hot(slot_column == iota((n_slots, n_faces), 1))
    net.send(0, lambda: dot(pick, t0.astype(BF16)).astype(BF16))

    ext = net.load(2)
    ext_row = jnp.concatenate([ext[f : f + 1] for f in range(6)], axis=1)
    ext_column = column(ext)
    perm_column = column(net.load(3)) + jnp.zeros((n_faces, LANES), jnp.int32)
    wall = ext_column + jnp.zeros((n_faces, LANES), jnp.int32) == n_faces + n_slots
    flip_r = (perm_column & 1) != 0
    flip_s = (perm_column & 2) != 0
    swap = (perm_column & 4) != 0
    base = faces.member * 16
    r, s = faces.node // 4, faces.node % 4
    r_old = jnp.where(swap, s, r)
    s_old = jnp.where(swap, r, s)
    r_old = jnp.where(flip_r, 3 - r_old, r_old)
    s_old = jnp.where(flip_s, 3 - s_old, s_old)
    unorient = base + 4 * r_old + s_old
    to_slots = one_hot(ext_row - n_faces == iota((n_slots, n_faces), 0))

    w = to_rows(net.load(4))
    w_jump = lift_factor * traces(w, elements)
    w_turned = lanes_of(jnp.where(wall, 0.0, w_jump), unorient)

    spare = faces.member >= 5

    def by_axis(x):
        signed = faces.sign * x
        tiles = [jnp.where(faces.axis == a, signed, 0.0) for a in range(3)]
        tiles[0] = jnp.where(spare, pltpu.roll(x, 80, 1), tiles[0])
        tiles[1] = jnp.where(spare, pltpu.roll(x, 32, 1), tiles[1])
        return jnp.concatenate(tiles, axis=1)

    def unpacked(x):
        tiles = [x[:, LANES * a : LANES * (a + 1)] for a in range(3)]
        plain = jnp.where(
            faces.member < 3,
            pltpu.roll(tiles[0], 48, 1),
            jnp.where(spare, 0.0, pltpu.roll(tiles[1], 96, 1)),
        )
        return [jnp.where(spare, 0.0, tiles[0]), jnp.where(spare, 0.0, tiles[1]), tiles[2], plain]

    cot_high, cot_low = halves(by_axis(w_turned))
    net.send(1, lambda: dot(to_slots, cot_high).astype(BF16))

    r_new = jnp.where(flip_r, 3 - r, r)
    s_new = jnp.where(flip_s, 3 - s, s)
    orient = base + jnp.where(swap, 4 * s_new + r_new, 4 * r_new + s_new)
    to_local = one_hot(ext_row == iota((n_faces, n_faces), 0))
    unpick = one_hot(slots == iota((n_faces, n_slots), 0))
    from_local = one_hot(ext_column == iota((n_faces, n_faces), 1))
    from_slots = one_hot(ext_column - n_faces == iota((n_faces, n_slots), 1))

    def outer_local(t):
        both = dot(from_local, jnp.concatenate(halves(t), axis=1))
        return both[:, :LANES] + both[:, LANES:]

    def outer(t, local, received):
        e = lanes_of(local + dot(from_slots, received), orient)
        return jnp.where(wall, t * faces.mirror, e)

    def half(t):
        return 0.5 * faces.flux(t) - t

    local0 = outer_local(t0)
    size = 3 * LANES
    mats = net.load(5)
    d_high, d_low = mats[:size], mats[size : 2 * size]
    b_high, b_low = (
        jnp.concatenate([mats[at + LANES * a : at + LANES * (a + 1)] for a in range(3)], axis=1)
        for at in (2 * size, 3 * size)
    )
    rate0 = volume(x0, d_high, d_low, elements)
    cot_local = dot(to_local, cot_high) + dot(to_local, cot_low) - by_axis(w_jump)
    slopes = dot_stacked(w, b_high, b_low)

    base0 = x0 + step_size * rate0
    half0 = half(t0)
    ready0 = faces.ready(t0)
    e0 = outer(t0, local0, net.wait(0))
    x1 = base0 + step_size * lift_factor * lift(half0 - half(e0), elements)
    t1 = traces(x1, elements)
    net.send(2, lambda: dot(pick, t1.astype(BF16)).astype(BF16))

    back1 = volume_back(x1, slopes, elements)
    wall_out = w_jump - 0.5 * faces.sign * faces.back(faces.ready(t1 * faces.mirror), w_jump)
    t_bar = jnp.where(wall, faces.mirror * wall_out, 0.0)
    ready1 = [faces.ready(t1, a) for a in range(3)]
    ready_e0 = faces.ready(e0)
    cot_all = unpacked(cot_local + dot(unpick, net.wait(1)))
    t_bar = t_bar + cot_all[3]
    for a in range(3):
        t_bar = t_bar - 0.5 * faces.back(ready1[a], cot_all[a], a)
    w1 = 0.5 * w + 0.5 * step_size * (back1 + lift(t_bar, elements))

    w1_jump = lift_factor * traces(w1, elements)
    out_bar = w1_jump - 0.5 * faces.sign * faces.back(ready_e0, w1_jump)
    turned = lanes_of(jnp.where(wall, 0.0, out_bar), unorient)
    turned_high, turned_low = halves(turned)
    net.send(3, lambda: dot(to_slots, turned_high).astype(BF16))

    in_bar = 0.5 * faces.sign * faces.back(ready0, w1_jump) - w1_jump
    in_bar = in_bar + jnp.where(wall, faces.mirror * out_bar, 0.0)
    in_bar = in_bar + dot(to_local, turned_high) + dot(to_local, turned_low)
    slopes1 = dot_stacked(w1, b_high, b_low)
    back0 = volume_back(x0, slopes1, elements)
    start = 0.5 * w + w1 + step_size * back0

    local1 = outer_local(t1)
    rate1 = volume(x1, d_high, d_low, elements)
    half1 = half(t1)
    e1 = outer(t1, local1, net.wait(2))
    rate1 = rate1 + lift_factor * lift(half1 - half(e1), elements)
    net.output(0, 0.5 * x0 + 0.5 * (x1 + step_size * rate1))
    net.sent((0, 1, 2))

    in_bar = in_bar + dot(unpick, net.wait(3))
    start = start + step_size * lift(in_bar, elements)
    net.output(1, start)


class Net:
    def __init__(
        self, n_dom, n_sub, inputs, held, send_bufs, recv_bufs, send_sem, recv_sem, load_sem
    ):
        self.n_dom, self.n_sub = n_dom, n_sub
        self.dom, self.sub = lax.axis_index("dom"), lax.axis_index("sub")
        self.send_bufs, self.recv_bufs = send_bufs, recv_bufs
        self.send_sem, self.recv_sem = send_sem, recv_sem
        self.greeted = False
        self.held = held
        self.loads = [
            pltpu.make_async_copy(inputs[n], held[n], load_sem.at[n]) for n in range(len(held))
        ]
        for load in self.loads:
            load.start()

    def load(self, which):
        self.loads[which].wait()
        return self.held[which][...]

    def partners(self, way=1):
        first = way * (2 * lax.rem(self.dom, 2) - 1)
        for group, ahead in ((1 + first, True), (1 - first, True), (1, False)):
            for j in range(self.n_sub):
                if ahead or j != 0:
                    yield group, lax.rem(self.sub + j, self.n_sub)

    def neighbour(self, steps):
        return lax.rem(self.dom + steps + self.n_dom, self.n_dom)

    def greet(self):
        barrier = pltpu.get_barrier_semaphore()
        for group, other in self.partners():
            pl.semaphore_signal(
                barrier,
                inc=1,
                device_id=(self.neighbour(group - 1), other),
                device_id_type=pl.DeviceIdType.MESH,
            )

    def copies(self, phase):
        source, target = self.send_bufs[phase], self.recv_bufs[phase]
        size = source.shape[0] // (3 * self.n_sub)
        way = 1 if phase % 2 == 0 else -1
        for group, other in self.partners(way):
            there = pl.multiple_of((group * self.n_sub + other) * size, size)
            here = pl.multiple_of((group * self.n_sub + self.sub) * size, size)
            yield pltpu.make_async_remote_copy(
                src_ref=source.at[pl.ds(there, size)],
                dst_ref=target.at[pl.ds(here, size)],
                send_sem=self.send_sem.at[phase, group * self.n_sub + other],
                recv_sem=self.recv_sem.at[phase, group * self.n_sub + self.sub],
                device_id=(self.neighbour(way * (group - 1)), other),
                device_id_type=pl.DeviceIdType.MESH,
            )

    def send(self, phase, make):
        source, target = self.send_bufs[phase], self.recv_bufs[phase]
        source[...] = make()
        if not self.greeted:
            pl.semaphore_wait(pltpu.get_barrier_semaphore(), 3 * self.n_sub - 1)
            self.greeted = True
        for copy in self.copies(phase):
            copy.start()
        size = source.shape[0] // (3 * self.n_sub)
        own = pl.ds(pl.multiple_of((self.n_sub + self.sub) * size, size), size)
        target[own] = source[own]

    def wait(self, phase):
        source, target = self.send_bufs[phase], self.recv_bufs[phase]
        size = source.shape[0] // (3 * self.n_sub)
        for group, other in self.partners():
            rows = pl.ds(pl.multiple_of((group * self.n_sub + other) * size, size), size)
            index = group * self.n_sub + other
            pltpu.make_async_remote_copy(
                src_ref=source.at[rows],
                dst_ref=target.at[rows],
                send_sem=self.send_sem.at[phase, index],
                recv_sem=self.recv_sem.at[phase, index],
                device_id=(self.neighbour(group - 1), other),
                device_id_type=pl.DeviceIdType.MESH,
            ).wait_recv()
        return target[...]

    def sent(self, phases):
        for phase in phases:
            for copy in self.copies(phase):
                copy.wait_send()

    def finish(self):
        self.sent((3,))
        for store in self.stores:
            store.wait()

    def output(self, which, x):
        elements = x.shape[0] // 3
        for member in range(5):
            tile, half = member // 2, member % 2
            self.staged[5 * which + member] = x[
                elements * tile : elements * (tile + 1), 64 * half : 64 * (half + 1)
            ]
        self.stores[which].start()


def kernel(n_dom, n_sub, *refs):
    inputs, out, held, staged = refs[:6], refs[6], refs[7:13], refs[13]
    send_bufs, recv_bufs = refs[14:18], refs[18:22]
    send_sem, recv_sem, load_sem, store_sem = refs[22:]
    net = Net(n_dom, n_sub, inputs, held, send_bufs, recv_bufs, send_sem, recv_sem, load_sem)
    net.staged = staged
    net.stores = [
        pltpu.make_async_copy(
            staged.at[pl.ds(5 * n, 5)], out.at[pl.ds(5 * n, 5)], store_sem.at[n]
        )
        for n in range(2)
    ]
    program(net)
    net.finish()


def hand_out(both, first, second, held, load_sems, store_sems):
    parts = [held.at[pl.ds(5 * n, 5)] for n in range(2)]
    loads = [
        pltpu.make_async_copy(both.at[pl.ds(5 * n, 5)], parts[n], load_sems.at[n])
        for n in range(2)
    ]
    stores = [
        pltpu.make_async_copy(parts[n], out, store_sems.at[n])
        for n, out in enumerate((first, second))
    ]
    for load in loads:
        load.start()
    for load, store in zip(loads, stores):
        load.wait()
        store.start()
    for store in stores:
        store.wait()


def solution(mesh):
    n_dom, n_sub = mesh.shape["dom"], mesh.shape["sub"]
    mats = constants()

    def shards(state, final, send_slot, ext_index, ext_perm):
        n_slots = send_slot.shape[1]
        widths = (LANES, 3 * LANES, LANES, LANES)
        buffers = [pltpu.VMEM((n_slots, width), BF16) for width in widths]
        operands = [
            state.transpose(0, 2, 1),
            send_slot,
            ext_index,
            ext_perm,
            final.transpose(0, 2, 1),
            jnp.asarray(mats),
        ]
        elements = state.shape[2]
        result = jax.ShapeDtypeStruct((10, elements, 64), F32)
        hbm = pl.BlockSpec(memory_space=pltpu.HBM)
        both = pl.pallas_call(
            lambda *refs: kernel(n_dom, n_sub, *refs),
            out_shape=result,
            in_specs=[hbm] * 6,
            out_specs=hbm,
            scratch_shapes=[pltpu.VMEM(x.shape, x.dtype) for x in operands]
            + [pltpu.VMEM((10, elements, 64), F32)]
            + buffers
            + buffers
            + [
                pltpu.SemaphoreType.DMA((4, 3 * n_sub)),
                pltpu.SemaphoreType.DMA((4, 3 * n_sub)),
                pltpu.SemaphoreType.DMA((6,)),
                pltpu.SemaphoreType.DMA((2,)),
            ],
            compiler_params=pltpu.CompilerParams(
                collective_id=0, has_side_effects=True, vmem_limit_bytes=60 * 1024 * 1024
            ),
        )(*operands)
        single = jax.ShapeDtypeStruct((5, elements, 64), F32)
        outs = pl.pallas_call(
            hand_out,
            out_shape=(single, single),
            in_specs=[hbm],
            out_specs=(hbm, hbm),
            scratch_shapes=[
                pltpu.VMEM((10, elements, 64), F32),
                pltpu.SemaphoreType.DMA((2,)),
                pltpu.SemaphoreType.DMA((2,)),
            ],
            compiler_params=pltpu.CompilerParams(vmem_limit_bytes=60 * 1024 * 1024),
        )(both)
        return tuple(x.transpose(0, 2, 1) for x in outs)

    return jax.shard_map(
        shards,
        mesh=mesh,
        in_specs=(
            P(None, None, ("dom", "sub")),
            P(None, None, ("dom", "sub")),
            P(("dom", "sub"), None),
            P(None, ("dom", "sub")),
            P(None, ("dom", "sub")),
        ),
        out_specs=(P(None, None, ("dom", "sub")), P(None, None, ("dom", "sub"))),
        check_vma=False,
    )
```
